128 devices in a mesh: tok: 4 (over x_hi, core), fin: 8 (over z, x_lo), fout: 4 (over y).
Axes of the slice: x: 4 (x_hi: 2, x_lo: 2; x = x_hi * 2 + x_lo), y: 4, z: 4, core: 2. Of those that a mesh axis runs over, the one named last changes fastest.
Arguments:
- inputs: bfloat16 [1024, 8192], P('tok', 'fin'), may hold values from -6 to 6
- upstream: bfloat16 [1024, 8192], P('tok', 'fin'), may hold values from -6 to 6
- loss_weight: int32 [1024], P('tok'), may hold values from 1 to 4
- pair_ids: int32 [1024], P('tok'), may hold values from 0 to 31
- margin: float32 [16], replicated, may hold values from -6 to 6
- w_gate: bfloat16 [8192, 16384], P('fin', ('tok', 'fout')), may hold values from -0.0625 to 0.0625
- w_up: bfloat16 [8192, 16384], P('fin', ('tok', 'fout')), may hold values from -0.0625 to 0.0625
- w_down: bfloat16 [16384, 8192], P(('tok', 'fout'), 'fin'), may hold values from -0.046875 to 0.046875
Outputs:
- grad_inputs: bfloat16 [1024, 8192], P(('tok', 'fout'), 'fin')
- grad_gate: bfloat16 [8192, 16384], P('fin', ('tok', 'fout'))
- grad_up: bfloat16 [8192, 16384], P('fin', ('tok', 'fout'))
- grad_down: bfloat16 [16384, 8192], P(('tok', 'fout'), 'fin')
The draws below stay inside these ranges and needn't reach their ends.
Inputs may be any that keep to these rules, and one draw needn't show every extreme that they name: pair_ids[t] // 2 is the pair of token t; even ids mark the chosen side, odd ids the rejected side.
All inputs are finite; a program needn't handle non-finite values.
Results may differ from the reference program's by a relative error of at most 0.0059.
Values may be sent and summed in bfloat16 or wider, within the bound.
No kernel may reach another device: no remote copies, remote signals or barrier semaphores. Data moves between devices by JAX's collectives and lax.ppermute only.
A program may use at most 128 MiB of HBM per device.

```python
import jax
import jax.numpy as jnp

D = 8192
F = 16384
PAIRS = 16
TOKENS = 1024


def touch_ends(drawn, key, smallest, largest):
    place = [jax.random.randint(jax.random.fold_in(key, axis), (), 0, length) for axis, length in enumerate(drawn.shape)]
    longest = drawn.shape.index(max(drawn.shape))
    beside = place[:longest] + [(place[longest] + 1) % drawn.shape[longest]] + place[longest + 1:]
    return drawn.at[tuple(place)].set(smallest).at[tuple(beside)].set(largest)


def steps_of(key, dims, split, smallest, high):
    level = 1.0
    for axis_at, parts in split:
        draws = jax.random.uniform(jax.random.fold_in(jax.random.fold_in(key, 6), axis_at), (parts,), jnp.float32, smallest / len(split), high / len(split))
        level = level * jnp.repeat(jnp.exp(draws), dims[axis_at] // parts).reshape((-1,) + (1,) * (len(dims) - 1 - axis_at))
    return level


def centred(stream_key, shape, spread, most, cuts=(), kind=jnp.bfloat16):
    array = spread * jax.random.normal(stream_key, shape, jnp.float32)
    if cuts:
        array = array * steps_of(stream_key, shape, cuts, -0.22, 0.18)
    return jnp.clip(array, -most, most).astype(kind)


def setup_inputs(seed: int = 0) -> dict:
    arg_keys = jax.random.split(jax.random.key(seed), 9)
    return {
        "inputs": centred(arg_keys[0], (TOKENS, D), 1.0, 6.0, ((0, 4), (1, 8))),
        "upstream": centred(arg_keys[1], (TOKENS, D), 1.0, 6.0, ((0, 4), (1, 8))),
        "loss_weight": touch_ends(jax.random.randint(arg_keys[2], (TOKENS,), 1, 5), jax.random.fold_in(arg_keys[2], 1), 1, 4).astype(jnp.int32),
        "pair_ids": touch_ends(jax.random.randint(arg_keys[3], (TOKENS,), 0, 2 * PAIRS), jax.random.fold_in(arg_keys[3], 1), 0, (2 * PAIRS) - 1).astype(jnp.int32),
        "margin": centred(arg_keys[4], (PAIRS,), 2.0, 6.0, (), jnp.float32),
        "w_gate": centred(arg_keys[5], (D, F), D ** -0.5, 0.0625, ((0, 8), (1, 16))),
        "w_up": centred(arg_keys[6], (D, F), D ** -0.5, 0.0625, ((0, 8), (1, 16))),
        "w_down": centred(arg_keys[7], (F, D), F ** -0.5, 0.046875, ((0, 16), (1, 8))),
    }


def reference(inputs, upstream, loss_weight, pair_ids, margin, w_gate, w_up, w_down):
    coefficient = jax.nn.sigmoid(-margin)
    side_table = jnp.stack([-coefficient, coefficient], axis=1).reshape(-1)
    row_scale = loss_weight.astype(jnp.float32) * side_table[pair_ids]
    grad_out = (row_scale[:, None] * upstream.astype(jnp.float32)).astype(jnp.bfloat16)
    pre_gate = jnp.dot(inputs, w_gate, preferred_element_type=jnp.float32)
    pre_up = jnp.dot(inputs, w_up, preferred_element_type=jnp.float32)
    grad_hidden = jnp.dot(grad_out, w_down.T, preferred_element_type=jnp.float32)
    sigmoid_gate = jax.nn.sigmoid(pre_gate)
    activated = pre_gate * sigmoid_gate
    hidden = (activated * pre_up).astype(jnp.bfloat16)
    grad_pre_gate = (grad_hidden * pre_up * sigmoid_gate * (1.0 + pre_gate * (1.0 - sigmoid_gate))).astype(jnp.bfloat16)
    grad_pre_up = (grad_hidden * activated).astype(jnp.bfloat16)
    grad_inputs = (jnp.dot(grad_pre_gate, w_gate.T, preferred_element_type=jnp.float32)
                   + jnp.dot(grad_pre_up, w_up.T, preferred_element_type=jnp.float32)).astype(jnp.bfloat16)
    grad_gate = jnp.dot(inputs.T, grad_pre_gate, preferred_element_type=jnp.float32).astype(jnp.bfloat16)
    grad_up = jnp.dot(inputs.T, grad_pre_up, preferred_element_type=jnp.float32).astype(jnp.bfloat16)
    grad_down = jnp.dot(hidden.T, grad_out, preferred_element_type=jnp.float32).astype(jnp.bfloat16)
    return grad_inputs, grad_gate, grad_up, grad_down
```

```python
import jax
import jax.numpy as jnp
from jax import lax
from jax.experimental import pallas as pl
from jax.experimental.pallas import tpu as pltpu
from jax.sharding import PartitionSpec as P

BF = jnp.bfloat16
F32 = jnp.float32
NT = (((1,), (1,)), ((), ()))
VMEM_LIMIT = 48 * 1024 * 1024


def params():
    return pltpu.CompilerParams(vmem_limit_bytes=VMEM_LIMIT)


def cost(flops, nbytes):
    return pl.CostEstimate(flops=flops, bytes_accessed=nbytes, transcendentals=0)


def fin_perm(x, dz, dx):
    pairs = [(z * 2 + l, ((z + dz) % 4) * 2 + (l ^ dx)) for z in range(4) for l in range(2)]
    return lax.ppermute(x, "fin", pairs)


def tok_perm(x, dh, dc):
    pairs = [(h * 2 + c, (h ^ dh) * 2 + (c ^ dc)) for h in range(2) for c in range(2)]
    return lax.ppermute(x, "tok", pairs)


def y_perm(x, dy):
    return lax.ppermute(x, "fout", [(y, (y + dy) % 4) for y in range(4)])


def row_start(z, lo, r, s):
    return pl.multiple_of((lax.rem(z + r, 4) * 2 + lax.bitwise_xor(lo, s)) * 32, 32)


def forward_kernel(idx, x, g, wg, wu, wd, plus, minus, keep, own, acc):
    z, lo = idx[0], idx[1]
    acc[0] = jnp.dot(x[...], wg[...], preferred_element_type=F32)
    acc[1] = jnp.dot(x[...], wu[...], preferred_element_type=F32)
    acc[2] = lax.dot_general(g[...], wd[...], NT, preferred_element_type=F32)

    def block(r, s):
        return acc[:, pl.ds(row_start(z, lo, r, s), 32), :]

    plus[0] = block(2, 0).astype(BF)
    plus[1] = block(1, 1).astype(BF)
    minus[0] = block(2, 1).astype(BF)
    minus[1] = block(3, 0).astype(BF)
    keep[0] = block(1, 0)
    keep[1] = block(3, 1)
    own[0] = block(0, 0)
    own[1] = block(0, 1)


def forward(idx, x, g, wg, wu, wd):
    tokens, depth = x.shape
    width = wg.shape[1]
    tile = 256
    full = pl.BlockSpec((tokens, depth), lambda i, s: (0, 0))
    part = pl.BlockSpec((2, 3, 32, tile), lambda i, s: (0, 0, 0, i))
    return pl.pallas_call(
        forward_kernel,
        grid_spec=pltpu.PrefetchScalarGridSpec(
            num_scalar_prefetch=1,
            grid=(width // tile,),
            in_specs=[
                full,
                full,
                pl.BlockSpec((depth, tile), lambda i, s: (0, i)),
                pl.BlockSpec((depth, tile), lambda i, s: (0, i)),
                pl.BlockSpec((tile, depth), lambda i, s: (i, 0)),
            ],
            out_specs=[part] * 4,
            scratch_shapes=[pltpu.VMEM((3, tokens, tile), F32)],
        ),
        out_shape=[
            jax.ShapeDtypeStruct((2, 3, 32, width), BF),
            jax.ShapeDtypeStruct((2, 3, 32, width), BF),
            jax.ShapeDtypeStruct((2, 3, 32, width), F32),
            jax.ShapeDtypeStruct((2, 3, 32, width), F32),
        ],
        compiler_params=params(),
        cost_estimate=cost(6 * tokens * depth * width, 6 * depth * width + 5 * 2**20),
        name="forward",
    )(idx, x, g, wg, wu, wd)


def pass_on_kernel(keep, from_minus, from_plus, plus, minus):
    plus[...] = (keep[0] + from_minus[0].astype(F32)).astype(BF)
    minus[...] = (keep[1] + from_plus[0].astype(F32)).astype(BF)


def pass_on(keep, from_minus, from_plus):
    shape = jax.ShapeDtypeStruct(keep.shape[1:], BF)
    return pl.pallas_call(
        pass_on_kernel,
        out_shape=[shape, shape],
        compiler_params=params(),
        cost_estimate=cost(keep.size, keep.size * 8),
        name="pass_on",
    )(keep, from_minus, from_plus)


def other_kernel(own, from_minus, last_plus, out):
    out[...] = (own[1] + from_minus[1].astype(F32) + last_plus[...].astype(F32)).astype(BF)


def other_half(own, from_minus, last_plus):
    return pl.pallas_call(
        other_kernel,
        out_shape=jax.ShapeDtypeStruct(own.shape[1:], BF),
        compiler_params=params(),
        cost_estimate=cost(own.size, own.size * 4),
        name="other_half",
    )(own, from_minus, last_plus)


def gate_kernel(own, from_plus, last_minus, across, out):
    total = own[0] + from_plus[1].astype(F32) + last_minus[...].astype(F32) + across[...].astype(F32)
    pre_gate, pre_up, grad_hidden = total[0], total[1], total[2]
    s = jax.nn.sigmoid(pre_gate)
    activated = pre_gate * s
    out[0] = (activated * pre_up).astype(BF)
    out[1] = (grad_hidden * pre_up * s * (1.0 + pre_gate * (1.0 - s))).astype(BF)
    out[2] = (grad_hidden * activated).astype(BF)


def gate(own, from_plus, last_minus, across):
    return pl.pallas_call(
        gate_kernel,
        out_shape=jax.ShapeDtypeStruct(own.shape[1:], BF),
        compiler_params=params(),
        cost_estimate=cost(own.size * 8, own.size * 5),
        name="gate",
    )(own, from_plus, last_minus, across)


def input_grad_kernel(idx, *refs):
    blocks, (wg, wu, plus, minus, keep, own, acts, acc) = refs[:8], refs[8:]
    z, lo, y = idx[0], idx[1], idx[2]

    @pl.when(pl.program_id(0) == 0)
    def _():
        for r in range(4):
            for s in range(2):
                acts[:, pl.ds(row_start(z, lo, r, s), 32), :] = blocks[2 * r + s][...]

    acc[...] = lax.dot_general(acts[1], wg[...], NT, preferred_element_type=F32) + lax.dot_general(
        acts[2], wu[...], NT, preferred_element_type=F32
    )

    def block(r, s):
        return acc[pl.ds(row_start(y, 0, r, s), 32), :]

    plus[0] = block(2, 0).astype(BF)
    plus[1] = block(1, 1).astype(BF)
    minus[0] = block(2, 1).astype(BF)
    minus[1] = block(3, 0).astype(BF)
    keep[0] = block(1, 0)
    keep[1] = block(3, 1)
    own[0] = block(0, 0)
    own[1] = block(0, 1)


def input_grad(idx, blocks, wg, wu):
    depth, width = wg.shape
    tile = 256
    part = pl.BlockSpec((2, 32, tile), lambda i, s: (0, 0, i))
    small = pl.BlockSpec((3, 32, width), lambda i, s: (0, 0, 0))
    weight = pl.BlockSpec((tile, width), lambda i, s: (i, 0))
    return pl.pallas_call(
        input_grad_kernel,
        grid_spec=pltpu.PrefetchScalarGridSpec(
            num_scalar_prefetch=1,
            grid=(depth // tile,),
            in_specs=[small] * 8 + [weight] * 2,
            out_specs=[part] * 4 + [pl.BlockSpec((3, 256, width), lambda i, s: (0, 0, 0))],
            scratch_shapes=[pltpu.VMEM((256, tile), F32)],
        ),
        out_shape=[
            jax.ShapeDtypeStruct((2, 32, depth), BF),
            jax.ShapeDtypeStruct((2, 32, depth), BF),
            jax.ShapeDtypeStruct((2, 32, depth), F32),
            jax.ShapeDtypeStruct((2, 32, depth), F32),
            jax.ShapeDtypeStruct((3, 256, width), BF),
        ],
        compiler_params=params(),
        cost_estimate=cost(4 * 256 * depth * width, 4 * depth * width + 4 * 2**20),
        name="input_grad",
    )(idx, *blocks, wg, wu)


def owned_kernel(own, from_minus, from_plus, last_minus, last_plus, out):
    out[0] = (own[0] + from_plus[1].astype(F32) + last_minus[...].astype(F32)).astype(out.dtype)
    out[1] = (own[1] + from_minus[1].astype(F32) + last_plus[...].astype(F32)).astype(out.dtype)


def owned(own, from_minus, from_plus, last_minus, last_plus, dtype):
    return pl.pallas_call(
        owned_kernel,
        out_shape=jax.ShapeDtypeStruct(own.shape, dtype),
        compiler_params=params(),
        cost_estimate=cost(own.size * 4, own.size * 10),
        name="owned",
    )(own, from_minus, from_plus, last_minus, last_plus)


def weight_grad_kernel(*refs):
    n = len(refs) // 3 - 1
    xs, gs, acts = refs[:n], refs[n : 2 * n], refs[2 * n : 3 * n]
    gate_out, up_out, down_out, xt = refs[3 * n :]

    @pl.when(pl.program_id(0) == 0)
    def _():
        for k in range(n):
            xt[:, k * 256 : (k + 1) * 256] = xs[k][...].T

    g = jnp.concatenate([r[...] for r in gs], axis=0)
    hidden = jnp.concatenate([r[0] for r in acts], axis=0)
    grad_gate = jnp.concatenate([r[1] for r in acts], axis=0)
    grad_up = jnp.concatenate([r[2] for r in acts], axis=0)
    gate_out[...] = jnp.dot(xt[...], grad_gate, preferred_element_type=F32).astype(BF)
    up_out[...] = jnp.dot(xt[...], grad_up, preferred_element_type=F32).astype(BF)
    down_out[...] = jnp.dot(hidden.T, g, preferred_element_type=F32).astype(BF)


def weight_grad(xs, gs, acts):
    tokens, depth = xs[0].shape
    width = acts[0].shape[2]
    n = len(xs)
    tile = 256
    full = pl.BlockSpec((tokens, depth), lambda i: (0, 0))
    return pl.pallas_call(
        weight_grad_kernel,
        grid=(width // tile,),
        in_specs=[full] * (2 * n) + [pl.BlockSpec((3, tokens, tile), lambda i: (0, 0, i))] * n,
        out_specs=[
            pl.BlockSpec((depth, tile), lambda i: (0, i)),
            pl.BlockSpec((depth, tile), lambda i: (0, i)),
            pl.BlockSpec((tile, depth), lambda i: (i, 0)),
        ],
        out_shape=[
            jax.ShapeDtypeStruct((depth, width), BF),
            jax.ShapeDtypeStruct((depth, width), BF),
            jax.ShapeDtypeStruct((width, depth), BF),
        ],
        scratch_shapes=[pltpu.VMEM((depth, n * tokens), BF)],
        compiler_params=params(),
        cost_estimate=cost(6 * n * tokens * depth * width, 16 * 2**20),
        name="weight_grad",
    )(*xs, *gs, *acts)


def body(inputs, upstream, loss_weight, pair_ids, margin, w_gate, w_up, w_down):
    fin = lax.axis_index("fin")
    idx = jnp.stack([fin // 2, fin % 2, lax.axis_index("fout")]).astype(jnp.int32)

    coefficient = jax.nn.sigmoid(-margin)
    side_table = jnp.stack([-coefficient, coefficient], axis=1).reshape(-1)
    columns = jnp.arange(side_table.shape[0], dtype=jnp.int32)
    picked = jnp.where(pair_ids[:, None] == columns[None, :], side_table[None, :], 0.0)
    row_scale = loss_weight.astype(F32) * jnp.sum(picked, axis=1)
    grad_out = (row_scale[:, None] * upstream.astype(F32)).astype(BF)

    x1, x2 = tok_perm(inputs, 0, 1), tok_perm(inputs, 1, 0)
    g1, g2 = tok_perm(grad_out, 0, 1), tok_perm(grad_out, 1, 0)
    x3, g3 = tok_perm(x2, 0, 1), tok_perm(g2, 0, 1)
    xs, gs = [inputs, x1, x2, x3], [grad_out, g1, g2, g3]

    acts, sums = [], []
    for k, offset in enumerate([(0, 0), (0, 1), (1, 0), (1, 1)]):
        plus, minus, keep, own = forward(idx, xs[k], gs[k], w_gate, w_up, w_down)
        from_minus, from_plus = fin_perm(plus, 1, 0), fin_perm(minus, 3, 0)
        plus, minus = pass_on(keep, from_minus, from_plus)
        last_minus, last_plus = fin_perm(plus, 1, 0), fin_perm(minus, 3, 0)
        across = fin_perm(other_half(own, from_minus, last_plus), 0, 1)
        mine = gate(own, from_plus, last_minus, across)

        theirs = fin_perm(mine, 0, 1)
        m_minus, m_plus = fin_perm(mine, 1, 0), fin_perm(mine, 3, 0)
        t_minus, t_plus = fin_perm(theirs, 1, 0), fin_perm(theirs, 3, 0)
        m_far, t_far = fin_perm(m_minus, 1, 0), fin_perm(t_plus, 3, 0)
        blocks = [mine, theirs, m_plus, t_plus, m_far, t_far, m_minus, t_minus]

        plus, minus, keep, own, act = input_grad(idx, blocks, w_gate, w_up)
        acts.append(act)
        from_minus, from_plus = y_perm(plus, 1), y_perm(minus, 3)
        plus, minus = pass_on(keep, from_minus, from_plus)
        last_minus, last_plus = y_perm(plus, 1), y_perm(minus, 3)
        part = owned(own, from_minus, from_plus, last_minus, last_plus, BF if k else F32)
        sums.append(tok_perm(part, *offset) if k else part)
    grad_gate, grad_up, grad_down = weight_grad(xs, gs, acts)
    total = sums[0] + sums[1].astype(F32) + sums[2].astype(F32) + sums[3].astype(F32)
    grad_inputs = total.astype(BF).reshape(-1, total.shape[-1])
    return (grad_inputs, grad_gate, grad_up, grad_down)


def solution(mesh):
    placed = (
        P("tok", "fin"),
        P("tok", "fin"),
        P("tok"),
        P("tok"),
        P(),
        P("fin", ("tok", "fout")),
        P("fin", ("tok", "fout")),
        P(("tok", "fout"), "fin"),
    )
    return jax.shard_map(
        body,
        mesh=mesh,
        in_specs=placed,
        out_specs=(
            P(("tok", "fout"), "fin"),
            P("fin", ("tok", "fout")),
            P("fin", ("tok", "fout")),
            P(("tok", "fout"), "fin"),
        ),
        check_vma=False,
    )
```

```python
import jax
import jax.numpy as jnp
from jax import lax
from jax.experimental import pallas as pl
from jax.experimental.pallas import tpu as pltpu
from jax.sharding import PartitionSpec as P

BF = jnp.bfloat16
F32 = jnp.float32
NT = (((1,), (1,)), ((), ()))
VMEM_LIMIT = 40 * 1024 * 1024


def params():
    return pltpu.CompilerParams(vmem_limit_bytes=VMEM_LIMIT)


def cost(flops, nbytes):
    return pl.CostEstimate(flops=flops, bytes_accessed=nbytes, transcendentals=0)


def fin_perm(x, dz, dx):
    pairs = [(z * 2 + l, ((z + dz) % 4) * 2 + (l ^ dx)) for z in range(4) for l in range(2)]
    return lax.ppermute(x, "fin", pairs)


def tok_perm(x, dh, dc):
    pairs = [(h * 2 + c, (h ^ dh) * 2 + (c ^ dc)) for h in range(2) for c in range(2)]
    return lax.ppermute(x, "tok", pairs)


def y_perm(x, dy):
    return lax.ppermute(x, "fout", [(y, (y + dy) % 4) for y in range(4)])


def row_start(z, lo, r, s):
    return pl.multiple_of((lax.rem(z + r, 4) * 2 + lax.bitwise_xor(lo, s)) * 32, 32)


def scale_kernel(margin, x, up, weight, ids, out):
    tokens = x.shape[0]
    out[0] = x[...]
    pair = ids[...] // 2
    picked = jnp.zeros(pair.shape, F32)
    for p in range(margin.shape[0]):
        picked = jnp.where(pair == p, margin[p], picked)
    side = jnp.where(ids[...] % 2 == 0, -1.0, 1.0)
    row = weight[...].astype(F32) * (side * jax.nn.sigmoid(-picked))
    at = lax.broadcasted_iota(jnp.int32, (tokens, tokens), 0)
    to = lax.broadcasted_iota(jnp.int32, (tokens, tokens), 1)
    column = jnp.sum(jnp.where(at == to, row, 0.0), axis=1, keepdims=True)
    out[1] = (column * up[...].astype(F32)).astype(BF)


def scaled(inputs, upstream, loss_weight, pair_ids, margin):
    tokens, depth = inputs.shape
    vmem = pl.BlockSpec(memory_space=pltpu.VMEM)
    return pl.pallas_call(
        scale_kernel,
        in_specs=[pl.BlockSpec(memory_space=pltpu.SMEM)] + [vmem] * 4,
        out_specs=vmem,
        out_shape=jax.ShapeDtypeStruct((2, tokens, depth), BF),
        compiler_params=params(),
        cost_estimate=cost(4 * tokens * depth, 8 * tokens * depth),
        name="scaled",
    )(margin, inputs, upstream, loss_weight.reshape(1, -1), pair_ids.reshape(1, -1))


def forward_kernel(idx, a, b, wg, wu, wd, plus, minus, keep, own, rows, acc):
    z, lo = idx[0], idx[1]
    tokens = a.shape[1]

    @pl.when(pl.program_id(0) == 0)
    def _():
        rows[:, :tokens] = a[...]
        rows[:, tokens:] = b[...]

    acc[0] = jnp.dot(rows[0], wg[...], preferred_element_type=F32)
    acc[1] = jnp.dot(rows[0], wu[...], preferred_element_type=F32)
    acc[2] = lax.dot_general(rows[1], wd[...], NT, preferred_element_type=F32)

    def put(out, k, r, s):
        start = row_start(z, lo, r, s)
        for t in range(2):
            out[k, :, t] = acc[:, pl.ds(t * tokens + start, 32), :].astype(out.dtype)

    put(plus, 0, 2, 0)
    put(plus, 1, 1, 1)
    put(minus, 0, 2, 1)
    put(minus, 1, 3, 0)
    put(keep, 0, 1, 0)
    put(keep, 1, 3, 1)
    put(own, 0, 0, 0)
    put(own, 1, 0, 1)


def forward(idx, a, b, wg, wu, wd):
    _, tokens, depth = a.shape
    width = wg.shape[1]
    tile = 256
    full = pl.BlockSpec((2, tokens, depth), lambda i, s: (0, 0, 0))
    part = pl.BlockSpec((2, 3, 2, 32, tile), lambda i, s: (0, 0, 0, 0, i))
    shape = (2, 3, 2, 32, width)
    return pl.pallas_call(
        forward_kernel,
        grid_spec=pltpu.PrefetchScalarGridSpec(
            num_scalar_prefetch=1,
            grid=(width // tile,),
            in_specs=[
                full,
                full,
                pl.BlockSpec((depth, tile), lambda i, s: (0, i)),
                pl.BlockSpec((depth, tile), lambda i, s: (0, i)),
                pl.BlockSpec((tile, depth), lambda i, s: (i, 0)),
            ],
            out_specs=[part] * 4,
            scratch_shapes=[
                pltpu.VMEM((2, 2 * tokens, depth), BF),
                pltpu.VMEM((3, 2 * tokens, tile), F32),
            ],
        ),
        out_shape=[
            jax.ShapeDtypeStruct(shape, BF),
            jax.ShapeDtypeStruct(shape, BF),
            jax.ShapeDtypeStruct(shape, F32),
            jax.ShapeDtypeStruct(shape, F32),
        ],
        compiler_params=params(),
        cost_estimate=cost(12 * tokens * depth * width, 6 * depth * width + 8 * 2**20),
        name="forward",
    )(idx, a, b, wg, wu, wd)


def pass_on_kernel(keep, from_minus, from_plus, plus, minus):
    plus[...] = (keep[0] + from_minus[0].astype(F32)).astype(BF)
    minus[...] = (keep[1] + from_plus[0].astype(F32)).astype(BF)


def pass_on(keep, from_minus, from_plus):
    shape = jax.ShapeDtypeStruct(keep.shape[1:], BF)
    return pl.pallas_call(
        pass_on_kernel,
        out_shape=[shape, shape],
        compiler_params=params(),
        cost_estimate=cost(keep.size, keep.size * 8),
        name="pass_on",
    )(keep, from_minus, from_plus)


def other_kernel(own, from_minus, last_plus, out):
    out[...] = (own[1] + from_minus[1].astype(F32) + last_plus[...].astype(F32)).astype(BF)


def other_half(own, from_minus, last_plus):
    return pl.pallas_call(
        other_kernel,
        out_shape=jax.ShapeDtypeStruct(own.shape[1:], BF),
        compiler_params=params(),
        cost_estimate=cost(own.size, own.size * 4),
        name="other_half",
    )(own, from_minus, last_plus)


def gate_kernel(own, from_plus, last_minus, across, out):
    total = own[0] + from_plus[1].astype(F32) + last_minus[...].astype(F32) + across[...].astype(F32)
    pre_gate, pre_up, grad_hidden = total[0], total[1], total[2]
    s = jax.nn.sigmoid(pre_gate)
    activated = pre_gate * s
    out[0] = (activated * pre_up).astype(BF)
    out[1] = (grad_hidden * pre_up * s * (1.0 + pre_gate * (1.0 - s))).astype(BF)
    out[2] = (grad_hidden * activated).astype(BF)


def gate(own, from_plus, last_minus, across):
    return pl.pallas_call(
        gate_kernel,
        out_shape=jax.ShapeDtypeStruct(own.shape[1:], BF),
        compiler_params=params(),
        cost_estimate=cost(own.size * 8, own.size * 5),
        name="gate",
    )(own, from_plus, last_minus, across)


def input_grad_kernel(idx, here, plus1, far_a, far_b, minus1, wg, wu, own, to1, to2, to3, acts, acc):
    z, lo, y = idx[0], idx[1], idx[2]
    tokens = acts.shape[1] // 2

    @pl.when(pl.program_id(0) == 0)
    def _():
        for r, s, block in (
            (0, 0, here.at[0]),
            (0, 1, here.at[1]),
            (1, 0, plus1.at[0]),
            (1, 1, plus1.at[1]),
            (2, 0, far_a),
            (2, 1, far_b),
            (3, 0, minus1.at[0]),
            (3, 1, minus1.at[1]),
        ):
            start = row_start(z, lo, r, s)
            for t in range(2):
                acts[:, pl.ds(t * tokens + start, 32), :] = block[:, t]

    acc[...] = lax.dot_general(acts[1], wg[...], NT, preferred_element_type=F32) + lax.dot_general(
        acts[2], wu[...], NT, preferred_element_type=F32
    )
    for r, out in enumerate((own, to1, to2, to3)):
        start = pl.multiple_of(lax.rem(y + r, 4) * 64, 64)
        for t in range(2):
            out[t] = acc[pl.ds(t * tokens + start, 64), :].astype(out.dtype)


def input_grad(idx, here, plus1, far_a, far_b, minus1, wg, wu):
    depth, width = wg.shape
    tokens = 256
    tile = 256
    part = pl.BlockSpec((2, 64, tile), lambda i, s: (0, 0, i))
    one = pl.BlockSpec((3, 2, 32, width), lambda i, s: (0, 0, 0, 0))
    two = pl.BlockSpec((2, 3, 2, 32, width), lambda i, s: (0, 0, 0, 0, 0))
    weight = pl.BlockSpec((tile, width), lambda i, s: (i, 0))
    return pl.pallas_call(
        input_grad_kernel,
        grid_spec=pltpu.PrefetchScalarGridSpec(
            num_scalar_prefetch=1,
            grid=(depth // tile,),
            in_specs=[two, two, one, one, two, weight, weight],
            out_specs=[part] * 4 + [pl.BlockSpec((3, 2 * tokens, width), lambda i, s: (0, 0, 0))],
            scratch_shapes=[pltpu.VMEM((2 * tokens, tile), F32)],
        ),
        out_shape=[
            jax.ShapeDtypeStruct((2, 64, depth), F32),
            jax.ShapeDtypeStruct((2, 64, depth), BF),
            jax.ShapeDtypeStruct((2, 64, depth), BF),
            jax.ShapeDtypeStruct((2, 64, depth), BF),
            jax.ShapeDtypeStruct((3, 2 * tokens, width), BF),
        ],
        compiler_params=params(),
        cost_estimate=cost(8 * tokens * depth * width, 4 * depth * width + 8 * 2**20),
        name="input_grad",
    )(idx, here, plus1, far_a, far_b, minus1, wg, wu)


def owned_kernel(own, a, b, c, mine, theirs):
    total = own[...] + a[...].astype(F32) + b[...].astype(F32) + c[...].astype(F32)
    mine[...] = total[0].astype(mine.dtype)
    theirs[...] = total[1].astype(BF)


def owned(own, a, b, c, dtype):
    return pl.pallas_call(
        owned_kernel,
        out_shape=[
            jax.ShapeDtypeStruct(own.shape[1:], dtype),
            jax.ShapeDtypeStruct(own.shape[1:], BF),
        ],
        compiler_params=params(),
        cost_estimate=cost(own.size * 4, own.size * 10),
        name="owned",
    )(own, a, b, c)


def weight_grad_kernel(*refs):
    rows, acts = refs[:4], refs[4:6]
    gate_out, up_out, down_out, xt, g = refs[6:]

    @pl.when(pl.program_id(0) == 0)
    def _():
        for k in range(4):
            xt[:, k * 256 : (k + 1) * 256] = rows[k][0].T
            g[k * 256 : (k + 1) * 256, :] = rows[k][1]

    hidden = jnp.concatenate([r[0] for r in acts], axis=0)
    grad_gate = jnp.concatenate([r[1] for r in acts], axis=0)
    grad_up = jnp.concatenate([r[2] for r in acts], axis=0)
    gate_out[...] = jnp.dot(xt[...], grad_gate, preferred_element_type=F32).astype(BF)
    up_out[...] = jnp.dot(xt[...], grad_up, preferred_element_type=F32).astype(BF)
    down_out[...] = jnp.dot(hidden.T, g[...], preferred_element_type=F32).astype(BF)


def weight_grad(rows, acts):
    _, tokens, depth = rows[0].shape
    width = acts[0].shape[2]
    tile = 256
    full = pl.BlockSpec((2, tokens, depth), lambda i: (0, 0, 0))
    return pl.pallas_call(
        weight_grad_kernel,
        grid=(width // tile,),
        in_specs=[full] * 4 + [pl.BlockSpec((3, 2 * tokens, tile), lambda i: (0, 0, i))] * 2,
        out_specs=[
            pl.BlockSpec((depth, tile), lambda i: (0, i)),
            pl.BlockSpec((depth, tile), lambda i: (0, i)),
            pl.BlockSpec((tile, depth), lambda i: (i, 0)),
        ],
        out_shape=[
            jax.ShapeDtypeStruct((depth, width), BF),
            jax.ShapeDtypeStruct((depth, width), BF),
            jax.ShapeDtypeStruct((width, depth), BF),
        ],
        scratch_shapes=[pltpu.VMEM((depth, 4 * tokens), BF), pltpu.VMEM((4 * tokens, depth), BF)],
        compiler_params=params(),
        cost_estimate=cost(24 * tokens * depth * width, 16 * 2**20),
        name="weight_grad",
    )(*rows, *acts)


def body(inputs, upstream, loss_weight, pair_ids, margin, w_gate, w_up, w_down):
    fin = lax.axis_index("fin")
    idx = jnp.stack([fin // 2, fin % 2, lax.axis_index("fout")]).astype(jnp.int32)

    m0 = scaled(inputs, upstream, loss_weight, pair_ids, margin)
    m1 = tok_perm(m0, 0, 1)
    m2 = tok_perm(m0, 1, 0)
    m3 = tok_perm(m2, 0, 1)

    acts, sums = [], []
    for k, (a, b) in enumerate(((m0, m1), (m2, m3))):
        plus, minus, keep, own = forward(idx, a, b, w_gate, w_up, w_down)
        from_minus, from_plus = fin_perm(plus, 1, 0), fin_perm(minus, 3, 0)
        plus, minus = pass_on(keep, from_minus, from_plus)
        last_minus, last_plus = fin_perm(plus, 1, 0), fin_perm(minus, 3, 0)
        across = fin_perm(other_half(own, from_minus, last_plus), 0, 1)
        mine = gate(own, from_plus, last_minus, across)

        here = jnp.stack([mine, fin_perm(mine, 0, 1)])
        minus1, plus1 = fin_perm(here, 1, 0), fin_perm(here, 3, 0)
        far_a, far_b = fin_perm(minus1[0], 1, 0), fin_perm(plus1[1], 3, 0)

        own, to1, to2, to3, act = input_grad(idx, here, plus1, far_a, far_b, minus1, w_gate, w_up)
        acts.append(act)
        a, b, c = y_perm(to1, 1), y_perm(to2, 2), y_perm(to3, 3)
        mine, theirs = owned(own, a, b, c, BF if k else F32)
        sums.append(tok_perm(mine, 1, 0) if k else mine)
        sums.append(tok_perm(theirs, k, 1))
    grad_gate, grad_up, grad_down = weight_grad((m0, m1, m2, m3), acts)
    total = sums[0] + sums[1].astype(F32) + sums[2].astype(F32) + sums[3].astype(F32)
    return (total.astype(BF), grad_gate, grad_up, grad_down)


def solution(mesh):
    placed = (
        P("tok", "fin"),
        P("tok", "fin"),
        P("tok"),
        P("tok"),
        P(),
        P("fin", ("tok", "fout")),
        P("fin", ("tok", "fout")),
        P(("tok", "fout"), "fin"),
    )
    return jax.shard_map(
        body,
        mesh=mesh,
        in_specs=placed,
        out_specs=(
            P(("tok", "fout"), "fin"),
            P("fin", ("tok", "fout")),
            P("fin", ("tok", "fout")),
            P(("tok", "fout"), "fin"),
        ),
        check_vma=False,
    )
```

```python
import jax
import jax.numpy as jnp
from jax import lax
from jax.experimental import pallas as pl
from jax.experimental.pallas import tpu as pltpu
from jax.sharding import PartitionSpec as P

BF = jnp.bfloat16
F32 = jnp.float32
NT = (((1,), (1,)), ((), ()))
VMEM_LIMIT = 16 * 1024 * 1024
PIPE_LIMIT = 24 * 1024 * 1024
SMEM = pl.BlockSpec(memory_space=pltpu.SMEM)
VMEM = pl.BlockSpec(memory_space=pltpu.VMEM)
WIDE_LIMIT = 56 * 1024 * 1024


def params(limit=VMEM_LIMIT):
    return pltpu.CompilerParams(vmem_limit_bytes=limit)


def cost(flops, nbytes):
    return pl.CostEstimate(flops=flops, bytes_accessed=nbytes, transcendentals=0)


def fin_perm(x, dz, dx):
    pairs = [(z * 2 + l, ((z + dz) % 4) * 2 + (l ^ dx)) for z in range(4) for l in range(2)]
    return lax.ppermute(x, "fin", pairs)


def tok_perm(x, dh, dc):
    pairs = [(h * 2 + c, (h ^ dh) * 2 + (c ^ dc)) for h in range(2) for c in range(2)]
    return lax.ppermute(x, "tok", pairs)


def y_perm(x, dy):
    return lax.ppermute(x, "fout", [(y, (y + dy) % 4) for y in range(4)])


def after(x, *done):
    n = len(x)
    return lax.optimization_barrier((*x, *done))[:n]


def row_start(z, lo, r, s):
    return pl.multiple_of((lax.rem(z + r, 4) * 2 + lax.bitwise_xor(lo, s)) * 32, 32)


def scale_kernel(margin, x, up, weight, ids, out):
    tokens = x.shape[0]
    out[0] = x[...]
    pair = ids[...] // 2
    picked = jnp.zeros(pair.shape, F32)
    for p in range(margin.shape[0]):
        picked = jnp.where(pair == p, margin[p], picked)
    side = jnp.where(ids[...] % 2 == 0, -1.0, 1.0)
    row = weight[...].astype(F32) * (side * jax.nn.sigmoid(-picked))
    at = lax.broadcasted_iota(jnp.int32, (tokens, tokens), 0)
    to = lax.broadcasted_iota(jnp.int32, (tokens, tokens), 1)
    column = jnp.sum(jnp.where(at == to, row, 0.0), axis=1, keepdims=True)
    out[1] = (column * up[...].astype(F32)).astype(BF)


def scaled(inputs, upstream, loss_weight, pair_ids, margin):
    tokens, depth = inputs.shape
    tile = depth // 2
    wide = pl.BlockSpec((tokens, tile), lambda i: (0, i))
    row = pl.BlockSpec((1, tokens), lambda i: (0, 0))
    return pl.pallas_call(
        scale_kernel,
        grid=(depth // tile,),
        in_specs=[pl.BlockSpec(memory_space=pltpu.SMEM), wide, wide, row, row],
        out_specs=pl.BlockSpec((2, tokens, tile), lambda i: (0, 0, i)),
        out_shape=jax.ShapeDtypeStruct((2, tokens, depth), BF),
        compiler_params=params(WIDE_LIMIT),
        cost_estimate=cost(4 * tokens * depth, 8 * tokens * depth),
        name="scaled",
    )(margin, inputs, upstream, loss_weight.reshape(1, -1), pair_ids.reshape(1, -1))


def forward_kernel(idx, m, wg, wu, wd, plus, minus, keep, own, acc):
    z, lo = idx[0], idx[1]
    tile = acc.shape[2]

    @pl.loop(0, wg.shape[1] // tile)
    def _(i):
        at = pl.ds(pl.multiple_of(i * tile, tile), tile)
        acc[0] = jnp.dot(m[0], wg[:, at], preferred_element_type=F32)
        acc[1] = jnp.dot(m[0], wu[:, at], preferred_element_type=F32)
        acc[2] = lax.dot_general(m[1], wd[at, :], NT, preferred_element_type=F32)

        def block(r, s):
            return acc[:, pl.ds(row_start(z, lo, r, s), 32), :]

        plus[0, :, :, at] = block(2, 0).astype(BF)
        plus[1, :, :, at] = block(1, 1).astype(BF)
        minus[0, :, :, at] = block(2, 1).astype(BF)
        minus[1, :, :, at] = block(3, 0).astype(BF)
        keep[0, :, :, at] = block(1, 0)
        keep[1, :, :, at] = block(3, 1)
        own[0, :, :, at] = block(0, 0)
        own[1, :, :, at] = block(0, 1)


def forward(idx, m, wg, wu, wd):
    _, tokens, depth = m.shape
    width = wg.shape[1]
    tile = 256
    shape = (2, 3, 32, width)
    return pl.pallas_call(
        forward_kernel,
        in_specs=[SMEM] + [VMEM] * 4,
        out_specs=[VMEM] * 4,
        out_shape=[
            jax.ShapeDtypeStruct(shape, BF),
            jax.ShapeDtypeStruct(shape, BF),
            jax.ShapeDtypeStruct(shape, F32),
            jax.ShapeDtypeStruct(shape, F32),
        ],
        scratch_shapes=[pltpu.VMEM((3, tokens, tile), F32)],
        compiler_params=params(),
        cost_estimate=cost(6 * tokens * depth * width, 5 * 2**20),
        name="forward",
    )(idx, m, wg, wu, wd)


def pass_on_kernel(*refs):
    plus, minus = refs[6:]
    for t in range(2):
        keep, from_minus, from_plus = refs[3 * t : 3 * t + 3]
        plus[:, t] = (keep[0] + from_minus[0].astype(F32)).astype(BF)
        minus[:, t] = (keep[1] + from_plus[0].astype(F32)).astype(BF)


def pass_on(keeps, nears):
    _, three, rows, width = keeps[0].shape
    shape = jax.ShapeDtypeStruct((three, 2, rows, width), BF)
    size = 2 * keeps[0].size
    return pl.pallas_call(
        pass_on_kernel,
        out_shape=[shape, shape],
        compiler_params=params(),
        cost_estimate=cost(size, size * 8),
        name="pass_on",
    )(keeps[0], *nears[:2], keeps[1], *nears[2:])


def ring_sum_kernel(*refs):
    last_minus, last_plus, held, sent = refs[6:]
    for t in range(2):
        own, from_minus, from_plus = refs[3 * t : 3 * t + 3]
        held[0, :, t] = own[0] + from_plus[1].astype(F32) + last_minus[:, t].astype(F32)
        held[1, :, t] = own[1] + from_minus[1].astype(F32) + last_plus[:, t].astype(F32)
    sent[...] = held[...].astype(BF)


def ring_sum(owns, nears, last_minus, last_plus):
    _, three, rows, width = owns[0].shape
    shape = (2, three, 2, rows, width)
    size = 2 * owns[0].size
    return pl.pallas_call(
        ring_sum_kernel,
        out_shape=[jax.ShapeDtypeStruct(shape, F32), jax.ShapeDtypeStruct(shape, BF)],
        compiler_params=params(),
        cost_estimate=cost(size * 4, size * 14),
        name="ring_sum",
    )(owns[0], *nears[:2], owns[1], *nears[2:], last_minus, last_plus)


def gate_kernel(held, across, out):
    for half in range(2):
        pre_gate, pre_up, grad_hidden = (
            held[half, i] + across[1 - half, i].astype(F32) for i in range(3)
        )
        s = jax.nn.sigmoid(pre_gate)
        activated = pre_gate * s
        out[half, 2] = (activated * pre_up).astype(BF)
        out[half, 0] = (grad_hidden * pre_up * s * (1.0 + pre_gate * (1.0 - s))).astype(BF)
        out[half, 1] = (grad_hidden * activated).astype(BF)


def gate(held, across):
    return pl.pallas_call(
        gate_kernel,
        out_shape=jax.ShapeDtypeStruct(held.shape, BF),
        compiler_params=params(),
        cost_estimate=cost(held.size * 8, held.size * 8),
        name="gate",
    )(held, across)


def input_grad_kernel(idx, here, plus1, far_a, far_b, minus1, wg, wu, own, to1, to2, to3, acts, acc):
    z, lo, y = idx[0], idx[1], idx[2]
    tokens = acts.shape[1] // 2
    tile = acc.shape[1]
    for r, s, block in (
        (0, 0, here.at[0]),
        (0, 1, here.at[1]),
        (1, 0, plus1.at[0]),
        (1, 1, plus1.at[1]),
        (2, 0, far_a),
        (2, 1, far_b),
        (3, 0, minus1.at[0]),
        (3, 1, minus1.at[1]),
    ):
        start = row_start(z, lo, r, s)
        for t in range(2):
            acts[:, pl.ds(t * tokens + start, 32), :] = block[:, t]

    @pl.loop(0, wg.shape[0] // tile)
    def _(i):
        at = pl.ds(pl.multiple_of(i * tile, tile), tile)
        acc[...] = lax.dot_general(acts[0], wg[at, :], NT, preferred_element_type=F32)
        acc[...] += lax.dot_general(acts[1], wu[at, :], NT, preferred_element_type=F32)
        for r, out in enumerate((own, to1, to2, to3)):
            start = pl.multiple_of(lax.rem(y + r, 4) * 64, 64)
            for t in range(2):
                out[t, :, at] = acc[pl.ds(t * tokens + start, 64), :].astype(out.dtype)


def input_grad(idx, here, plus1, far_a, far_b, minus1, wg, wu):
    depth, width = wg.shape
    tokens = 256
    tile = 256
    return pl.pallas_call(
        input_grad_kernel,
        in_specs=[SMEM] + [VMEM] * 7,
        out_specs=[VMEM] * 5,
        out_shape=[
            jax.ShapeDtypeStruct((2, 64, depth), F32),
            jax.ShapeDtypeStruct((2, 64, depth), BF),
            jax.ShapeDtypeStruct((2, 64, depth), BF),
            jax.ShapeDtypeStruct((2, 64, depth), BF),
            jax.ShapeDtypeStruct((3, 2 * tokens, width), BF),
        ],
        scratch_shapes=[pltpu.VMEM((2 * tokens, tile), F32)],
        compiler_params=params(),
        cost_estimate=cost(8 * tokens * depth * width, 10 * 2**20),
        name="input_grad",
    )(idx, here, plus1, far_a, far_b, minus1, wg, wu)


def owned_kernel(own0, a0, b0, c0, own1, a1, b1, c1, mine, core, far, cross):
    first = own0[...] + a0[...].astype(F32) + b0[...].astype(F32) + c0[...].astype(F32)
    last = own1[...] + a1[...].astype(F32) + b1[...].astype(F32) + c1[...].astype(F32)
    mine[...] = first[0]
    core[...] = first[1].astype(BF)
    far[...] = last[0].astype(BF)
    cross[...] = last[1].astype(BF)


def owned(first, last):
    shape = first[0].shape[1:]
    small = jax.ShapeDtypeStruct(shape, BF)
    return pl.pallas_call(
        owned_kernel,
        out_shape=[jax.ShapeDtypeStruct(shape, F32), small, small, small],
        compiler_params=params(),
        cost_estimate=cost(first[0].size * 8, first[0].size * 20),
        name="owned",
    )(*first, *last)


def in_grads_kernel(*refs):
    rows, acts, before, (gate_out, up_out, xt) = refs[:2], refs[2], refs[3:-3], refs[-3:]

    @pl.when(pl.program_id(0) == 0)
    def _():
        for k in range(2):
            xt[:, k * 256 : (k + 1) * 256] = rows[k][0].T

    for k, out in enumerate((gate_out, up_out)):
        total = jnp.dot(xt[...], acts[k], preferred_element_type=F32)
        if before:
            total += before[k][...]
        out[...] = total.astype(out.dtype)


def in_grads(rows, acts, before, dtype):
    _, tokens, depth = rows[0].shape
    width = acts.shape[2]
    tile = 256
    full = pl.BlockSpec((1, tokens, depth), lambda i: (0, 0, 0))
    part = pl.BlockSpec((depth, tile), lambda i: (0, i))
    out = jax.ShapeDtypeStruct((depth, width), dtype)
    return pl.pallas_call(
        in_grads_kernel,
        grid=(width // tile,),
        in_specs=[full] * 2
        + [pl.BlockSpec((2, 2 * tokens, tile), lambda i: (0, 0, i))]
        + [part] * len(before),
        out_specs=[part] * 2,
        out_shape=[out, out],
        scratch_shapes=[pltpu.VMEM((depth, 2 * tokens), BF)],
        compiler_params=params(PIPE_LIMIT),
        cost_estimate=cost(8 * tokens * depth * width, 12 * 2**20),
        name="in_grads",
    )(*rows, acts, *before)


def down_grad_kernel(*refs):
    rows, acts = refs[:4], refs[4:6]
    out, g = refs[6:]

    @pl.when(pl.program_id(0) == 0)
    def _():
        for k in range(4):
            g[k * 256 : (k + 1) * 256, :] = rows[k][0]

    hidden = jnp.concatenate([r[0] for r in acts], axis=0)
    out[...] = jnp.dot(hidden.T, g[...], preferred_element_type=F32).astype(BF)


def down_grad(rows, acts):
    _, tokens, depth = rows[0].shape
    width = acts[0].shape[2]
    tile = 256
    full = pl.BlockSpec((1, tokens, depth), lambda i: (1, 0, 0))
    return pl.pallas_call(
        down_grad_kernel,
        grid=(width // tile,),
        in_specs=[full] * 4 + [pl.BlockSpec((1, 2 * tokens, tile), lambda i: (2, 0, i))] * 2,
        out_specs=pl.BlockSpec((tile, depth), lambda i: (i, 0)),
        out_shape=jax.ShapeDtypeStruct((width, depth), BF),
        scratch_shapes=[pltpu.VMEM((4 * tokens, depth), BF)],
        compiler_params=params(PIPE_LIMIT),
        cost_estimate=cost(8 * tokens * depth * width, 6 * 2**20),
        name="down_grad",
    )(*rows, *acts)


def body(inputs, upstream, loss_weight, pair_ids, margin, w_gate, w_up, w_down):
    fin = lax.axis_index("fin")
    idx = jnp.stack([fin // 2, fin % 2, lax.axis_index("fout")]).astype(jnp.int32)

    m0 = scaled(inputs, upstream, loss_weight, pair_ids, margin)
    m1 = tok_perm(m0, 0, 1)
    m2 = tok_perm(m0, 1, 0)

    def ring(plus, minus):
        return fin_perm(plus, 1, 0), fin_perm(minus, 3, 0)

    def over_y(own, to1, to2, to3):
        return own, y_perm(to1, 1), y_perm(to2, 2), y_perm(to3, 3)

    weights = w_gate, w_up, w_down
    *out, keep_a, own_a = forward(idx, m0, *weights)
    near_a = ring(*out)
    (m1,) = after((m1,), *out)
    *out, keep_b, own_b = forward(idx, m1, *weights)
    near0 = *near_a, *ring(*out)
    owns0 = own_a, own_b
    step0 = pass_on((keep_a, keep_b), near0)
    last0 = ring(*step0)

    (m2,) = after((m2,), *step0)
    m3 = tok_perm(m2, 0, 1)
    *out, keep_a, own_a = forward(idx, m2, *weights)
    near_a = ring(*out)
    last0 = after(last0, *out)
    held0, sent0 = ring_sum(owns0, near0, *last0)
    across0 = fin_perm(sent0, 0, 1)
    (m3,) = after((m3,), sent0)
    *out, keep_b, own_b = forward(idx, m3, *weights)
    near1 = *near_a, *ring(*out)
    step1 = pass_on((keep_a, keep_b), near1)
    last1 = ring(*step1)

    (across0,) = after((across0,), *step1)
    here0 = gate(held0, across0)
    last1 = after(last1, here0)
    held1, sent1 = ring_sum((own_a, own_b), near1, *last1)
    across1 = fin_perm(sent1, 0, 1)

    (ready,) = after((here0,), sent1)
    minus1, plus1 = ring(ready, ready)
    on_plus, on_minus = minus1[0], plus1[1]
    far0 = ring(on_plus, on_minus)
    (across1,) = after((across1,), on_plus, on_minus)
    here1 = gate(held1, across1)
    side1 = ring(here1, here1)

    far0 = after(far0, here1)
    *grad0, act0 = input_grad(idx, here0, plus1, *far0, minus1, w_gate, w_up)
    first = over_y(*grad0)
    before = in_grads((m0, m1), act0, (), F32)

    minus1, plus1 = after(side1, *before)
    far1 = ring(minus1[0], plus1[1])
    *grad1, act1 = input_grad(idx, here1, plus1, *far1, minus1, w_gate, w_up)
    last = over_y(*grad1)

    grad_gate, grad_up = in_grads((m2, m3), act1, before, BF)
    rows = after((m0, m1, m2, m3), grad_gate)
    grad_down = down_grad(rows, (act0, act1))
    parts = after((*first, *last), grad_down)
    mine, core, far_part, cross = owned(parts[:4], parts[4:])
    others = (tok_perm(core, 0, 1), tok_perm(far_part, 1, 0), tok_perm(cross, 1, 1))
    total = mine + sum(r.astype(F32) for r in others)
    return (total.astype(BF), grad_gate, grad_up, grad_down)


def solution(mesh):
    placed = (
        P("tok", "fin"),
        P("tok", "fin"),
        P("tok"),
        P("tok"),
        P(),
        P("fin", ("tok", "fout")),
        P("fin", ("tok", "fout")),
        P(("tok", "fout"), "fin"),
    )
    return jax.shard_map(
        body,
        mesh=mesh,
        in_specs=placed,
        out_specs=(
            P(("tok", "fout"), "fin"),
            P("fin", ("tok", "fout")),
            P("fin", ("tok", "fout")),
            P(("tok", "fout"), "fin"),
        ),
        check_vma=False,
    )
```

```python
import jax
import jax.numpy as jnp
from jax import lax
from jax.experimental import pallas as pl
from jax.experimental.pallas import tpu as pltpu
from jax.sharding import PartitionSpec as P

BF = jnp.bfloat16
F32 = jnp.float32
NT = (((1,), (1,)), ((), ()))
VMEM_LIMIT = 16 * 1024 * 1024
FIRST_LIMIT = 56 * 1024 * 1024
SMEM = pl.BlockSpec(memory_space=pltpu.SMEM)
VMEM = pl.BlockSpec(memory_space=pltpu.VMEM)


def params(limit=VMEM_LIMIT):
    return pltpu.CompilerParams(vmem_limit_bytes=limit)


def cost(flops, nbytes):
    return pl.CostEstimate(flops=flops, bytes_accessed=nbytes, transcendentals=0)


def fin_perm(x, dz, dx):
    pairs = [(z * 2 + l, ((z + dz) % 4) * 2 + (l ^ dx)) for z in range(4) for l in range(2)]
    return lax.ppermute(x, "fin", pairs)


def tok_perm(x, dh, dc):
    pairs = [(h * 2 + c, (h ^ dh) * 2 + (c ^ dc)) for h in range(2) for c in range(2)]
    return lax.ppermute(x, "tok", pairs)


def y_perm(x, dy):
    return lax.ppermute(x, "fout", [(y, (y + dy) % 4) for y in range(4)])


def after(x, *done):
    n = len(x)
    return lax.optimization_barrier((*x, *done))[:n]


def row_start(z, lo, r, s):
    return pl.multiple_of((lax.rem(z + r, 4) * 2 + lax.bitwise_xor(lo, s)) * 32, 32)


def scale_kernel(margin, x, up, weight, ids, out):
    tokens = x.shape[0]
    out[0] = x[...]
    pair = ids[...] // 2
    picked = jnp.zeros(pair.shape, F32)
    for p in range(margin.shape[0]):
        picked = jnp.where(pair == p, margin[p], picked)
    side = jnp.where(ids[...] % 2 == 0, -1.0, 1.0)
    row = weight[...].astype(F32) * (side * jax.nn.sigmoid(-picked))
    at = lax.broadcasted_iota(jnp.int32, (tokens, tokens), 0)
    to = lax.broadcasted_iota(jnp.int32, (tokens, tokens), 1)
    column = jnp.sum(jnp.where(at == to, row, 0.0), axis=1, keepdims=True)
    out[1] = (column * up[...].astype(F32)).astype(BF)


def scaled(inputs, upstream, loss_weight, pair_ids, margin):
    tokens, depth = inputs.shape
    tile = depth // 2
    wide = pl.BlockSpec((tokens, tile), lambda i: (0, i))
    row = pl.BlockSpec((1, tokens), lambda i: (0, 0))
    return pl.pallas_call(
        scale_kernel,
        grid=(depth // tile,),
        in_specs=[pl.BlockSpec(memory_space=pltpu.SMEM), wide, wide, row, row],
        out_specs=pl.BlockSpec((2, tokens, tile), lambda i: (0, 0, i)),
        out_shape=jax.ShapeDtypeStruct((2, tokens, depth), BF),
        compiler_params=params(FIRST_LIMIT),
        cost_estimate=cost(4 * tokens * depth, 8 * tokens * depth),
        name="scaled",
    )(margin, inputs, upstream, loss_weight.reshape(1, -1), pair_ids.reshape(1, -1))


def forward_kernel(idx, m, wg, wu, wd, plus, minus, keep, own, acc):
    z, lo = idx[0], idx[1]
    tile = acc.shape[2]

    @pl.loop(0, wg.shape[1] // tile)
    def _(i):
        at = pl.ds(pl.multiple_of(i * tile, tile), tile)
        acc[0] = jnp.dot(m[0], wg[:, at], preferred_element_type=F32)
        acc[1] = jnp.dot(m[0], wu[:, at], preferred_element_type=F32)
        acc[2] = lax.dot_general(m[1], wd[at, :], NT, preferred_element_type=F32)

        def block(r, s):
            return acc[:, pl.ds(row_start(z, lo, r, s), 32), :]

        plus[0, :, :, at] = block(2, 0).astype(BF)
        plus[1, :, :, at] = block(1, 1).astype(BF)
        minus[0, :, :, at] = block(2, 1).astype(BF)
        minus[1, :, :, at] = block(3, 0).astype(BF)
        keep[0, :, :, at] = block(1, 0)
        keep[1, :, :, at] = block(3, 1)
        own[0, :, :, at] = block(0, 0)
        own[1, :, :, at] = block(0, 1)


def forward(idx, m, wg, wu, wd):
    _, tokens, depth = m.shape
    width = wg.shape[1]
    tile = 256
    shape = (2, 3, 32, width)
    return pl.pallas_call(
        forward_kernel,
        in_specs=[SMEM] + [VMEM] * 4,
        out_specs=[VMEM] * 4,
        out_shape=[
            jax.ShapeDtypeStruct(shape, BF),
            jax.ShapeDtypeStruct(shape, BF),
            jax.ShapeDtypeStruct(shape, F32),
            jax.ShapeDtypeStruct(shape, F32),
        ],
        scratch_shapes=[pltpu.VMEM((3, tokens, tile), F32)],
        compiler_params=params(),
        cost_estimate=cost(6 * tokens * depth * width, 5 * 2**20),
        name="forward",
    )(idx, m, wg, wu, wd)


def pass_on_kernel(*refs):
    plus, minus = refs[6:]
    for t in range(2):
        keep, from_minus, from_plus = refs[3 * t : 3 * t + 3]
        plus[:, t] = (keep[0] + from_minus[0].astype(F32)).astype(BF)
        minus[:, t] = (keep[1] + from_plus[0].astype(F32)).astype(BF)


def pass_on(keeps, nears):
    _, three, rows, width = keeps[0].shape
    shape = jax.ShapeDtypeStruct((three, 2, rows, width), BF)
    size = 2 * keeps[0].size
    return pl.pallas_call(
        pass_on_kernel,
        out_shape=[shape, shape],
        compiler_params=params(),
        cost_estimate=cost(size, size * 8),
        name="pass_on",
    )(keeps[0], *nears[:2], keeps[1], *nears[2:])


def ring_sum_kernel(*refs):
    last_minus, last_plus, held, sent = refs[6:]
    for t in range(2):
        own, from_minus, from_plus = refs[3 * t : 3 * t + 3]
        held[0, :, t] = own[0] + from_plus[1].astype(F32) + last_minus[:, t].astype(F32)
        held[1, :, t] = own[1] + from_minus[1].astype(F32) + last_plus[:, t].astype(F32)
    sent[...] = held[...].astype(BF)


def ring_sum(owns, nears, last_minus, last_plus):
    _, three, rows, width = owns[0].shape
    shape = (2, three, 2, rows, width)
    size = 2 * owns[0].size
    return pl.pallas_call(
        ring_sum_kernel,
        out_shape=[jax.ShapeDtypeStruct(shape, F32), jax.ShapeDtypeStruct(shape, BF)],
        compiler_params=params(),
        cost_estimate=cost(size * 4, size * 14),
        name="ring_sum",
    )(owns[0], *nears[:2], owns[1], *nears[2:], last_minus, last_plus)


def gate_kernel(held, across, out, other):
    for half in range(2):
        pre_gate, pre_up, grad_hidden = (
            held[half, i] + across[1 - half, i].astype(F32) for i in range(3)
        )
        s = jax.nn.sigmoid(pre_gate)
        activated = pre_gate * s
        first = 6 * half
        out[first : first + 2] = (
            grad_hidden * pre_up * s * (1.0 + pre_gate * (1.0 - s))
        ).astype(BF)
        out[first + 2 : first + 4] = (grad_hidden * activated).astype(BF)
        hidden = (activated * pre_up).astype(BF)
        if half:
            other[...] = hidden
        else:
            out[4:6] = hidden


def gate(held, across):
    _, _, two, rows, width = held.shape
    return pl.pallas_call(
        gate_kernel,
        in_specs=[VMEM] * 2,
        out_specs=[VMEM] * 2,
        out_shape=[
            jax.ShapeDtypeStruct((10, rows, width), BF),
            jax.ShapeDtypeStruct((two, rows, width), BF),
        ],
        compiler_params=params(),
        cost_estimate=cost(held.size * 8, held.size * 8),
        name="gate",
    )(held, across)


def input_grad_kernel(idx, here, plus1, far_a, far_b, minus1, wg, wu, mine, theirs, acts, hidden, acc):
    z, lo = idx[0], idx[1]
    tokens = acts.shape[1] // 2
    tile = acc.shape[1]
    for r, s, block in (
        (0, 0, here.at[:4]),
        (0, 1, here.at[6:]),
        (1, 0, plus1.at[:4]),
        (1, 1, plus1.at[6:]),
        (2, 0, far_a.at[:4]),
        (2, 1, far_b.at[1:]),
        (3, 0, minus1.at[:4]),
        (3, 1, minus1.at[6:]),
    ):
        start = row_start(z, lo, r, s)
        for i in range(2):
            for t in range(2):
                acts[i, pl.ds(t * tokens + start, 32), :] = block[2 * i + t]
    hidden[0] = plus1[4:6]
    hidden[1, 0] = far_a[4]
    hidden[1, 1] = far_b[0]
    hidden[2] = minus1[4:6]

    @pl.loop(0, wg.shape[0] // tile)
    def _(i):
        at = pl.ds(pl.multiple_of(i * tile, tile), tile)
        acc[...] = lax.dot_general(acts[0], wg[at, :], NT, preferred_element_type=F32)
        acc[...] += lax.dot_general(acts[1], wu[at, :], NT, preferred_element_type=F32)
        mine[:, at] = acc[:tokens]
        theirs[:, at] = acc[tokens:].astype(BF)


def input_grad(idx, here, plus1, far_a, far_b, minus1, wg, wu):
    depth, width = wg.shape
    tokens = 256
    tile = 256
    return pl.pallas_call(
        input_grad_kernel,
        in_specs=[SMEM] + [VMEM] * 7,
        out_specs=[VMEM] * 4,
        out_shape=[
            jax.ShapeDtypeStruct((tokens, depth), F32),
            jax.ShapeDtypeStruct((tokens, depth), BF),
            jax.ShapeDtypeStruct((2, 2 * tokens, width), BF),
            jax.ShapeDtypeStruct((3, 2, 32, width), BF),
        ],
        scratch_shapes=[pltpu.VMEM((2 * tokens, tile), F32)],
        compiler_params=params(),
        cost_estimate=cost(8 * tokens * depth * width, 10 * 2**20),
        name="input_grad",
    )(idx, here, plus1, far_a, far_b, minus1, wg, wu)


def split_kernel(idx, mine, across, *outs):
    for r, out in enumerate(outs):
        at = pl.ds(pl.multiple_of(lax.rem(idx[2] + r, 4) * 64, 64), 64)
        out[...] = (mine[at, :] + across[at, :].astype(F32)).astype(out.dtype)


def split(idx, mine, across):
    shape = (64, mine.shape[1])
    return pl.pallas_call(
        split_kernel,
        in_specs=[SMEM, VMEM, VMEM],
        out_specs=[VMEM] * 4,
        out_shape=[jax.ShapeDtypeStruct(shape, F32)] + [jax.ShapeDtypeStruct(shape, BF)] * 3,
        compiler_params=params(),
        cost_estimate=cost(mine.size, mine.size * 9),
        name="split",
    )(idx, mine, across)


def owned_kernel(own, a, b, c, out):
    total = own[...] + a[...].astype(F32) + b[...].astype(F32) + c[...].astype(F32)
    out[...] = total.astype(out.dtype)


def owned(own, a, b, c, dtype):
    return pl.pallas_call(
        owned_kernel,
        in_specs=[VMEM] * 4,
        out_specs=VMEM,
        out_shape=jax.ShapeDtypeStruct(own.shape, dtype),
        compiler_params=params(),
        cost_estimate=cost(own.size * 4, own.size * 12),
        name="owned",
    )(own, a, b, c)


def part_grads_kernel(m0, m1, acts, gate_out, up_out, xt):
    tokens = m0.shape[1]
    for k, m in enumerate((m0, m1)):
        xt[:, k * tokens : (k + 1) * tokens] = m[0].T
    tile = 256

    @pl.loop(0, acts.shape[2] // tile)
    def _(i):
        at = pl.ds(pl.multiple_of(i * tile, tile), tile)
        gate_out[:, at] = jnp.dot(xt[...], acts[0, :, at], preferred_element_type=F32)
        up_out[:, at] = jnp.dot(xt[...], acts[1, :, at], preferred_element_type=F32)


def part_grads(m0, m1, acts):
    _, tokens, depth = m0.shape
    width = acts.shape[2]
    out = jax.ShapeDtypeStruct((depth, width), F32)
    return pl.pallas_call(
        part_grads_kernel,
        in_specs=[VMEM] * 3,
        out_specs=[VMEM] * 2,
        out_shape=[out, out],
        scratch_shapes=[pltpu.VMEM((depth, 2 * tokens), BF)],
        compiler_params=params(),
        cost_estimate=cost(8 * tokens * depth * width, 8 * 2**20),
        name="part_grads",
    )(m0, m1, acts)


def in_grads_kernel(m0, m1, acts, gate_part, up_part, gate_out, up_out, xt):
    tokens = m0.shape[1]
    tile = gate_out.shape[1]
    i = pl.program_id(0)

    @pl.when(i == 0)
    def _():
        for k, m in enumerate((m0, m1)):
            xt[:, k * tokens : (k + 1) * tokens] = m[0].T

    at = pl.ds(pl.multiple_of(i * tile, tile), tile)
    total = gate_part[:, at] + jnp.dot(xt[...], acts[0, :, at], preferred_element_type=F32)
    gate_out[...] = total.astype(BF)
    total = up_part[:, at] + jnp.dot(xt[...], acts[1, :, at], preferred_element_type=F32)
    up_out[...] = total.astype(BF)


def in_grads(m0, m1, acts, gate_part, up_part):
    _, tokens, depth = m0.shape
    width = acts.shape[2]
    tile = 256
    out = jax.ShapeDtypeStruct((depth, width), BF)
    return pl.pallas_call(
        in_grads_kernel,
        grid=(width // tile,),
        in_specs=[VMEM] * 5,
        out_specs=[pl.BlockSpec((depth, tile), lambda i: (0, i))] * 2,
        out_shape=[out, out],
        scratch_shapes=[pltpu.VMEM((depth, 2 * tokens), BF)],
        compiler_params=params(),
        cost_estimate=cost(8 * tokens * depth * width, 8 * 2**20),
        name="in_grads",
    )(m0, m1, acts, gate_part, up_part)


def gather_hidden(idx, here, other, near, across, out, base):
    for r in range(4):
        for s in range(2):
            start = row_start(idx[0], idx[1], r, s)
            for t in range(2):
                if r:
                    block = (across if s else near)[r - 1, t]
                else:
                    block = other[t] if s else here[4 + t]
                out[pl.ds(base + t * 256 + start, 32), :] = block


def down_grad_kernel(idx, *refs):
    rows, blocks, (out, hidden) = refs[:4], refs[4:12], refs[12:]
    tile = out.shape[0]
    i = pl.program_id(0)

    @pl.when(i == 0)
    def _():
        for k in range(2):
            gather_hidden(idx, *blocks[4 * k : 4 * k + 4], hidden, k * 512)

    at = pl.ds(pl.multiple_of(i * tile, tile), tile)
    g = jnp.concatenate([m[1] for m in rows], axis=0)
    total = jnp.dot(hidden[:, at].T, g, preferred_element_type=F32)
    out[...] = total.astype(BF)


def down_grad(idx, rows, blocks0, blocks1):
    _, tokens, depth = rows[0].shape
    width = blocks0[0].shape[2]
    tile = 256
    return pl.pallas_call(
        down_grad_kernel,
        grid=(width // tile,),
        in_specs=[SMEM] + [VMEM] * 12,
        out_specs=pl.BlockSpec((tile, depth), lambda i: (i, 0)),
        out_shape=jax.ShapeDtypeStruct((width, depth), BF),
        scratch_shapes=[pltpu.VMEM((4 * tokens, width), BF)],
        compiler_params=params(),
        cost_estimate=cost(8 * tokens * depth * width, 4 * 2**20),
        name="down_grad",
    )(idx, *rows, *blocks0, *blocks1)


def body(inputs, upstream, loss_weight, pair_ids, margin, w_gate, w_up, w_down):
    fin = lax.axis_index("fin")
    idx = jnp.stack([fin // 2, fin % 2, lax.axis_index("fout")]).astype(jnp.int32)

    weights = w_gate, w_up, w_down
    m0 = scaled(inputs, upstream, loss_weight, pair_ids, margin)
    m1 = tok_perm(m0, 0, 1)
    m2 = tok_perm(m0, 1, 0)

    def ring(plus, minus):
        return fin_perm(plus, 1, 0), fin_perm(minus, 3, 0)

    def over_y(own, to1, to2, to3):
        return own, y_perm(to1, 1), y_perm(to2, 2), y_perm(to3, 3)

    *out, keep_a, own_a = forward(idx, m0, *weights)
    near_a = ring(*out)
    (m1,) = after((m1,), *out)
    *out, keep_b, own_b = forward(idx, m1, *weights)
    near0 = *near_a, *ring(*out)
    owns0 = own_a, own_b
    step0 = pass_on((keep_a, keep_b), near0)
    last0 = ring(*step0)

    (m2,) = after((m2,), *step0)
    m3 = tok_perm(m2, 0, 1)
    *out, keep_a, own_a = forward(idx, m2, *weights)
    near_a = ring(*out)
    last0 = after(last0, *out)
    held0, sent0 = ring_sum(owns0, near0, *last0)
    across0 = fin_perm(sent0, 0, 1)
    (m3,) = after((m3,), sent0)
    *out, keep_b, own_b = forward(idx, m3, *weights)
    near1 = *near_a, *ring(*out)
    step1 = pass_on((keep_a, keep_b), near1)
    last1 = ring(*step1)

    (across0,) = after((across0,), *step1)
    here0, other0 = gate(held0, across0)
    last1 = after(last1, here0)
    held1, sent1 = ring_sum((own_a, own_b), near1, *last1)
    across1 = fin_perm(sent1, 0, 1)

    (ready,) = after((here0,), sent1)
    minus1, plus1 = ring(ready, ready)
    on_plus, on_minus = minus1[:5], plus1[5:]
    far0 = ring(on_plus, on_minus)
    (across1,) = after((across1,), on_plus, on_minus)
    here1, other1 = gate(held1, across1)
    side1 = ring(here1, here1)

    far0 = after(far0, here1)
    mine0, theirs0, act0, near = input_grad(idx, here0, plus1, *far0, minus1, *weights[:2])
    core0 = tok_perm(theirs0, 0, 1)
    blocks0 = here0, other0, near, fin_perm(near, 0, 1)
    gate_part, up_part = part_grads(m0, m1, act0)
    (core0,) = after((core0,), gate_part)
    parts0 = split(idx, mine0, core0)
    sums0 = over_y(*parts0)
    side1 = after(side1, parts0[0])
    far1 = ring(side1[0][:5], side1[1][5:])

    far1 = after(far1, *sums0[1:], blocks0[3])
    mine1, theirs1, act1, near = input_grad(idx, here1, side1[1], *far1, side1[0], *weights[:2])
    core1 = tok_perm(theirs1, 0, 1)
    blocks1 = here1, other1, near, fin_perm(near, 0, 1)
    total0 = owned(*after(sums0, act1), F32)
    (core1,) = after((core1,), total0)
    parts1 = split(idx, mine1, core1)
    sums1 = over_y(*parts1)
    (act1,) = after((act1,), parts1[0])
    grad_gate, grad_up = in_grads(m2, m3, act1, gate_part, up_part)
    far = owned(*after(sums1, grad_gate), BF)
    blocks1 = after(blocks1, far)
    far = tok_perm(far, 1, 0)
    grad_down = down_grad(idx, (m0, m1, m2, m3), blocks0, blocks1)
    (far,) = after((far,), grad_down)
    total = total0 + far.astype(F32)
    return (total.astype(BF), grad_gate, grad_up, grad_down)


def solution(mesh):
    placed = (
        P("tok", "fin"),
        P("tok", "fin"),
        P("tok"),
        P("tok"),
        P(),
        P("fin", ("tok", "fout")),
        P("fin", ("tok", "fout")),
        P(("tok", "fout"), "fin"),
    )
    return jax.shard_map(
        body,
        mesh=mesh,
        in_specs=placed,
        out_specs=(
            P(("tok", "fout"), "fin"),
            P("fin", ("tok", "fout")),
            P("fin", ("tok", "fout")),
            P(("tok", "fout"), "fin"),
        ),
        check_vma=False,
    )
```

```python
import jax
import jax.numpy as jnp
from jax import lax
from jax.experimental import pallas as pl
from jax.experimental.pallas import tpu as pltpu
from jax.sharding import PartitionSpec as P

BF = jnp.bfloat16
F32 = jnp.float32
NT = (((1,), (1,)), ((), ()))
VMEM_LIMIT = 16 * 1024 * 1024
FIRST_LIMIT = 56 * 1024 * 1024
SMEM = pl.BlockSpec(memory_space=pltpu.SMEM)
VMEM = pl.BlockSpec(memory_space=pltpu.VMEM)


def params(limit=VMEM_LIMIT):
    return pltpu.CompilerParams(vmem_limit_bytes=limit)


def cost(flops, nbytes):
    return pl.CostEstimate(flops=flops, bytes_accessed=nbytes, transcendentals=0)


def fin_perm(x, dz, dx):
    pairs = [(z * 2 + l, ((z + dz) % 4) * 2 + (l ^ dx)) for z in range(4) for l in range(2)]
    return lax.ppermute(x, "fin", pairs)


def tok_perm(x, dh, dc):
    pairs = [(h * 2 + c, (h ^ dh) * 2 + (c ^ dc)) for h in range(2) for c in range(2)]
    return lax.ppermute(x, "tok", pairs)


def y_perm(x, dy):
    return lax.ppermute(x, "fout", [(y, (y + dy) % 4) for y in range(4)])


def after(x, *done):
    n = len(x)
    return lax.optimization_barrier((*x, *done))[:n]


def row_start(z, lo, r, s):
    return pl.multiple_of((lax.rem(z + r, 4) * 2 + lax.bitwise_xor(lo, s)) * 32, 32)


def scale_kernel(margin, x, up, weight, ids, out):
    tokens = x.shape[0]
    out[0] = x[...]
    pair = ids[...] // 2
    picked = jnp.zeros(pair.shape, F32)
    for p in range(margin.shape[0]):
        picked = jnp.where(pair == p, margin[p], picked)
    side = jnp.where(ids[...] % 2 == 0, -1.0, 1.0)
    row = weight[...].astype(F32) * (side * jax.nn.sigmoid(-picked))
    at = lax.broadcasted_iota(jnp.int32, (tokens, tokens), 0)
    to = lax.broadcasted_iota(jnp.int32, (tokens, tokens), 1)
    column = jnp.sum(jnp.where(at == to, row, 0.0), axis=1, keepdims=True)
    out[1] = (column * up[...].astype(F32)).astype(BF)


def scaled(inputs, upstream, loss_weight, pair_ids, margin):
    tokens, depth = inputs.shape
    tile = depth // 2
    wide = pl.BlockSpec((tokens, tile), lambda i: (0, i))
    row = pl.BlockSpec((1, tokens), lambda i: (0, 0))
    return pl.pallas_call(
        scale_kernel,
        grid=(depth // tile,),
        in_specs=[pl.BlockSpec(memory_space=pltpu.SMEM), wide, wide, row, row],
        out_specs=pl.BlockSpec((2, tokens, tile), lambda i: (0, 0, i)),
        out_shape=jax.ShapeDtypeStruct((2, tokens, depth), BF),
        compiler_params=params(FIRST_LIMIT),
        cost_estimate=cost(4 * tokens * depth, 8 * tokens * depth),
        name="scaled",
    )(margin, inputs, upstream, loss_weight.reshape(1, -1), pair_ids.reshape(1, -1))


def forward_kernel(idx, m, wg, wu, wd, plus, minus, keep, own, acc):
    z, lo = idx[0], idx[1]
    tile = acc.shape[2]

    @pl.loop(0, wg.shape[1] // tile)
    def _(i):
        at = pl.ds(pl.multiple_of(i * tile, tile), tile)
        acc[0] = jnp.dot(m[0], wg[:, at], preferred_element_type=F32)
        acc[1] = jnp.dot(m[0], wu[:, at], preferred_element_type=F32)
        acc[2] = lax.dot_general(m[1], wd[at, :], NT, preferred_element_type=F32)

        def block(r, s):
            return acc[:, pl.ds(row_start(z, lo, r, s), 32), :]

        plus[0, :, :, at] = block(2, 0).astype(BF)
        plus[1, :, :, at] = block(1, 1).astype(BF)
        minus[0, :, :, at] = block(2, 1).astype(BF)
        minus[1, :, :, at] = block(3, 0).astype(BF)
        keep[0, :, :, at] = block(1, 0)
        keep[1, :, :, at] = block(3, 1)
        own[0, :, :, at] = block(0, 0)
        own[1, :, :, at] = block(0, 1)


def forward(idx, m, wg, wu, wd):
    _, tokens, depth = m.shape
    width = wg.shape[1]
    tile = 256
    shape = (2, 3, 32, width)
    return pl.pallas_call(
        forward_kernel,
        in_specs=[SMEM] + [VMEM] * 4,
        out_specs=[VMEM] * 4,
        out_shape=[
            jax.ShapeDtypeStruct(shape, BF),
            jax.ShapeDtypeStruct(shape, BF),
            jax.ShapeDtypeStruct(shape, F32),
            jax.ShapeDtypeStruct(shape, F32),
        ],
        scratch_shapes=[pltpu.VMEM((3, tokens, tile), F32)],
        compiler_params=params(),
        cost_estimate=cost(6 * tokens * depth * width, 5 * 2**20),
        name="forward",
    )(idx, m, wg, wu, wd)


def own_forward_kernel(idx, m, wg, wu, wd, plus, minus, keep, own, hg, hu, acc, sems):
    z, lo = idx[0], idx[1]
    piece = 256
    order = [(k, i) for i in range(wg.shape[0] // piece) for k in range(2)]
    places = (wg, hg), (wu, hu)
    copies = []
    for n, (k, i) in enumerate(order):
        src, dst = places[k]
        at = pl.ds(i * piece, piece)
        copies.append(pltpu.make_async_copy(src.at[at], dst.at[at], sems.at[n]))
    ahead = 4
    for copy in copies[:ahead]:
        copy.start()
    acc[2] = lax.dot_general(m[1], wd[...], NT, preferred_element_type=F32)
    for n, (k, i) in enumerate(order):
        copies[n].wait()
        if n + ahead < len(copies):
            copies[n + ahead].start()
        at = slice(i * piece, (i + 1) * piece)
        part = jnp.dot(m[0, :, at], places[k][1][at, :], preferred_element_type=F32)
        acc[k] = acc[k] + part if i else part

    def block(r, s):
        return acc[:, pl.ds(row_start(z, lo, r, s), 32), :]

    plus[0] = block(2, 0).astype(BF)
    plus[1] = block(1, 1).astype(BF)
    minus[0] = block(2, 1).astype(BF)
    minus[1] = block(3, 0).astype(BF)
    keep[0] = block(1, 0)
    keep[1] = block(3, 1)
    own[0] = block(0, 0)
    own[1] = block(0, 1)


def own_forward(idx, m, wg, wu, wd):
    _, tokens, depth = m.shape
    width = wg.shape[1]
    shape = (2, 3, 32, width)
    return pl.pallas_call(
        own_forward_kernel,
        in_specs=[SMEM, VMEM] + [pl.BlockSpec(memory_space=pl.ANY)] * 2 + [VMEM],
        out_specs=[VMEM] * 4,
        out_shape=[
            jax.ShapeDtypeStruct(shape, BF),
            jax.ShapeDtypeStruct(shape, BF),
            jax.ShapeDtypeStruct(shape, F32),
            jax.ShapeDtypeStruct(shape, F32),
        ],
        scratch_shapes=[
            pltpu.VMEM(wg.shape, BF),
            pltpu.VMEM(wu.shape, BF),
            pltpu.VMEM((3, tokens, width), F32),
            pltpu.SemaphoreType.DMA((8,)),
        ],
        compiler_params=params(50 * 2**20),
        cost_estimate=cost(6 * tokens * depth * width, 11 * 2**20),
        name="own_forward",
    )(idx, m, wg, wu, wd)


def pass_on_kernel(*refs):
    plus, minus = refs[6:]
    for t in range(2):
        keep, from_minus, from_plus = refs[3 * t : 3 * t + 3]
        plus[:, t] = (keep[0] + from_minus[0].astype(F32)).astype(BF)
        minus[:, t] = (keep[1] + from_plus[0].astype(F32)).astype(BF)


def pass_on(keeps, nears):
    _, three, rows, width = keeps[0].shape
    shape = jax.ShapeDtypeStruct((three, 2, rows, width), BF)
    size = 2 * keeps[0].size
    return pl.pallas_call(
        pass_on_kernel,
        out_shape=[shape, shape],
        compiler_params=params(),
        cost_estimate=cost(size, size * 8),
        name="pass_on",
    )(keeps[0], *nears[:2], keeps[1], *nears[2:])


def ring_sum_kernel(*refs):
    last_minus, last_plus, held, sent = refs[6:]
    for t in range(2):
        own, from_minus, from_plus = refs[3 * t : 3 * t + 3]
        held[0, :, t] = own[0] + from_plus[1].astype(F32) + last_minus[:, t].astype(F32)
        held[1, :, t] = own[1] + from_minus[1].astype(F32) + last_plus[:, t].astype(F32)
    sent[...] = held[...].astype(BF)


def ring_sum(owns, nears, last_minus, last_plus):
    _, three, rows, width = owns[0].shape
    shape = (2, three, 2, rows, width)
    size = 2 * owns[0].size
    return pl.pallas_call(
        ring_sum_kernel,
        out_shape=[jax.ShapeDtypeStruct(shape, F32), jax.ShapeDtypeStruct(shape, BF)],
        compiler_params=params(),
        cost_estimate=cost(size * 4, size * 14),
        name="ring_sum",
    )(owns[0], *nears[:2], owns[1], *nears[2:], last_minus, last_plus)


def cross_forward_kernel(idx, m, wg, wu, wd, plus, minus, keep, own, cross, stay, acc):
    z, lo = idx[0], idx[1]
    tile = acc.shape[2]

    @pl.loop(0, wg.shape[1] // tile)
    def _(i):
        at = pl.ds(pl.multiple_of(i * tile, tile), tile)
        acc[0] = jnp.dot(m[0], wg[:, at], preferred_element_type=F32)
        acc[1] = jnp.dot(m[0], wu[:, at], preferred_element_type=F32)
        acc[2] = lax.dot_general(m[1], wd[at, :], NT, preferred_element_type=F32)

        def block(r, s):
            return acc[:2, pl.ds(row_start(z, lo, r, s), 32), :]

        plus[0, :, :, at] = block(2, 0).astype(BF)
        plus[1, :, :, at] = block(1, 1).astype(BF)
        minus[0, :, :, at] = block(2, 1).astype(BF)
        minus[1, :, :, at] = block(3, 0).astype(BF)
        keep[0, :, :, at] = block(1, 0)
        keep[1, :, :, at] = block(3, 1)
        own[0, :, :, at] = block(0, 0)
        own[1, :, :, at] = block(0, 1)
        for r in range(4):
            stay[r, :, at] = acc[2, pl.ds(row_start(z, lo, r, 0), 32), :]
            cross[r, :, at] = acc[2, pl.ds(row_start(z, lo, r, 1), 32), :].astype(BF)


def cross_forward(idx, m, wg, wu, wd):
    _, tokens, depth = m.shape
    width = wg.shape[1]
    tile = 256
    shape = (2, 2, 32, width)
    return pl.pallas_call(
        cross_forward_kernel,
        in_specs=[SMEM] + [VMEM] * 4,
        out_specs=[VMEM] * 6,
        out_shape=[
            jax.ShapeDtypeStruct(shape, BF),
            jax.ShapeDtypeStruct(shape, BF),
            jax.ShapeDtypeStruct(shape, F32),
            jax.ShapeDtypeStruct(shape, F32),
            jax.ShapeDtypeStruct((4, 32, width), BF),
            jax.ShapeDtypeStruct((4, 32, width), F32),
        ],
        scratch_shapes=[pltpu.VMEM((3, tokens, tile), F32)],
        compiler_params=params(),
        cost_estimate=cost(6 * tokens * depth * width, 5 * 2**20),
        name="cross_forward",
    )(idx, m, wg, wu, wd)


def cross_sum_kernel(stay0, got0, stay1, got1, plus, minus, keep, own):
    def total(t, r):
        stay, got = (stay0, got0) if t == 0 else (stay1, got1)
        return stay[r] + got[r].astype(F32)

    plus[0] = total(0, 2).astype(BF)
    plus[1] = total(1, 1).astype(BF)
    minus[0] = total(1, 2).astype(BF)
    minus[1] = total(0, 3).astype(BF)
    keep[0] = total(0, 1)
    keep[1] = total(1, 3)
    own[0] = total(0, 0)
    own[1] = total(1, 0)


def cross_sum(stay0, got0, stay1, got1):
    shape = (2, *stay0.shape[1:])
    return pl.pallas_call(
        cross_sum_kernel,
        in_specs=[VMEM] * 4,
        out_specs=[VMEM] * 4,
        out_shape=[
            jax.ShapeDtypeStruct(shape, BF),
            jax.ShapeDtypeStruct(shape, BF),
            jax.ShapeDtypeStruct(shape, F32),
            jax.ShapeDtypeStruct(shape, F32),
        ],
        compiler_params=params(),
        cost_estimate=cost(stay0.size * 2, stay0.size * 18),
        name="cross_sum",
    )(stay0, got0, stay1, got1)


def cross_pass_on_kernel(*refs):
    (keep, from_minus, from_plus), (plus, minus) = refs[6:9], refs[9:]
    plus[4] = (keep[0] + from_minus[0].astype(F32)).astype(BF)
    minus[4] = (keep[1] + from_plus[0].astype(F32)).astype(BF)
    for t in range(2):
        keep, from_minus, from_plus = refs[3 * t : 3 * t + 3]
        for i in range(2):
            plus[2 * i + t] = (keep[0, i] + from_minus[0, i].astype(F32)).astype(BF)
            minus[2 * i + t] = (keep[1, i] + from_plus[0, i].astype(F32)).astype(BF)


def cross_pass_on(keeps, nears):
    _, _, rows, width = keeps[0].shape
    shape = jax.ShapeDtypeStruct((5, rows, width), BF)
    size = 10 * rows * width
    return pl.pallas_call(
        cross_pass_on_kernel,
        in_specs=[VMEM] * 9,
        out_specs=[VMEM] * 2,
        out_shape=[shape, shape],
        compiler_params=params(),
        cost_estimate=cost(size, size * 8),
        name="cross_pass_on",
    )(keeps[0], *nears[:2], keeps[1], *nears[2:4], keeps[2], *nears[4:])


def cross_ring_sum_kernel(*refs):
    (own_g, minus_g, plus_g), (last_minus, last_plus, held, held_g, sent) = refs[6:9], refs[9:]
    for t in range(2):
        own, from_minus, from_plus = refs[3 * t : 3 * t + 3]
        for i in range(2):
            k = 2 * i + t
            held[k] = own[0, i] + from_plus[1, i].astype(F32) + last_minus[k].astype(F32)
            held[4 + k] = own[1, i] + from_minus[1, i].astype(F32) + last_plus[k].astype(F32)
    held_g[0] = own_g[0] + plus_g[1].astype(F32) + last_minus[4].astype(F32)
    held_g[1] = own_g[1] + minus_g[1].astype(F32) + last_plus[4].astype(F32)
    sent[:8] = held[...].astype(BF)
    sent[8:] = held_g[...].astype(BF)


def cross_ring_sum(owns, nears, last_minus, last_plus):
    _, _, rows, width = owns[0].shape
    size = 10 * rows * width
    return pl.pallas_call(
        cross_ring_sum_kernel,
        in_specs=[VMEM] * 11,
        out_specs=[VMEM] * 3,
        out_shape=[
            jax.ShapeDtypeStruct((8, rows, width), F32),
            jax.ShapeDtypeStruct((2, rows, width), F32),
            jax.ShapeDtypeStruct((10, rows, width), BF),
        ],
        compiler_params=params(),
        cost_estimate=cost(size * 4, size * 14),
        name="cross_ring_sum",
    )(owns[0], *nears[:2], owns[1], *nears[2:4], owns[2], *nears[4:], last_minus, last_plus)


def cross_gate_kernel(held, held_g, across, out, other):
    for half in range(2):
        mine, theirs = 4 * half, 4 * (1 - half)
        pre_gate = held[mine : mine + 2] + across[theirs : theirs + 2].astype(F32)
        pre_up = held[mine + 2 : mine + 4] + across[theirs + 2 : theirs + 4].astype(F32)
        grad_hidden = across[8:].astype(F32) if half else held_g[...]
        put_gate(half, pre_gate, pre_up, grad_hidden, out, other)


def cross_gate(held, held_g, across):
    _, rows, width = held.shape
    return pl.pallas_call(
        cross_gate_kernel,
        in_specs=[VMEM] * 3,
        out_specs=[VMEM] * 2,
        out_shape=[
            jax.ShapeDtypeStruct((10, rows, width), BF),
            jax.ShapeDtypeStruct((2, rows, width), BF),
        ],
        compiler_params=params(),
        cost_estimate=cost(held.size * 8, held.size * 8),
        name="cross_gate",
    )(held, held_g, across)


def put_gate(half, pre_gate, pre_up, grad_hidden, out, other):
    s = jax.nn.sigmoid(pre_gate)
    activated = pre_gate * s
    first = 6 * half
    out[first : first + 2] = (
        grad_hidden * pre_up * s * (1.0 + pre_gate * (1.0 - s))
    ).astype(BF)
    out[first + 2 : first + 4] = (grad_hidden * activated).astype(BF)
    hidden = (activated * pre_up).astype(BF)
    if half:
        other[...] = hidden
    else:
        out[4:6] = hidden


def gate_kernel(held, across, out, other):
    for half in range(2):
        pre_gate, pre_up, grad_hidden = (
            held[half, i] + across[1 - half, i].astype(F32) for i in range(3)
        )
        put_gate(half, pre_gate, pre_up, grad_hidden, out, other)


def gate(held, across):
    _, _, two, rows, width = held.shape
    return pl.pallas_call(
        gate_kernel,
        in_specs=[VMEM] * 2,
        out_specs=[VMEM] * 2,
        out_shape=[
            jax.ShapeDtypeStruct((10, rows, width), BF),
            jax.ShapeDtypeStruct((two, rows, width), BF),
        ],
        compiler_params=params(),
        cost_estimate=cost(held.size * 8, held.size * 8),
        name="gate",
    )(held, across)


def their_grad_kernel(idx, here, plus1, far_a, far_b, minus1, wg, wu, theirs, acts, hidden):
    z, lo = idx[0], idx[1]
    tokens = acts.shape[1] // 2
    for r, s, block in (
        (0, 0, here.at[:4]),
        (0, 1, here.at[6:]),
        (1, 0, plus1.at[:4]),
        (1, 1, plus1.at[6:]),
        (2, 0, far_a.at[:4]),
        (2, 1, far_b.at[1:]),
        (3, 0, minus1.at[:4]),
        (3, 1, minus1.at[6:]),
    ):
        start = row_start(z, lo, r, s)
        for i in range(2):
            for t in range(2):
                acts[i, pl.ds(t * tokens + start, 32), :] = block[2 * i + t]
    hidden[0] = plus1[4:6]
    hidden[1, 0] = far_a[4]
    hidden[1, 1] = far_b[0]
    hidden[2] = minus1[4:6]

    rows_grad(acts, tokens, wg, wu, theirs)


def rows_grad(acts, first, wg, wu, out):
    rows, tile = out.shape[0], 256

    @pl.loop(0, wg.shape[0] // tile)
    def _(i):
        at = pl.ds(pl.multiple_of(i * tile, tile), tile)
        total = lax.dot_general(
            acts[0, first : first + rows], wg[at, :], NT, preferred_element_type=F32
        )
        total += lax.dot_general(
            acts[1, first : first + rows], wu[at, :], NT, preferred_element_type=F32
        )
        out[:, at] = total.astype(out.dtype)


def their_grad(idx, here, plus1, far_a, far_b, minus1, wg, wu):
    depth, width = wg.shape
    tokens = 256
    return pl.pallas_call(
        their_grad_kernel,
        in_specs=[SMEM] + [VMEM] * 7,
        out_specs=[VMEM] * 3,
        out_shape=[
            jax.ShapeDtypeStruct((tokens, depth), BF),
            jax.ShapeDtypeStruct((2, 2 * tokens, width), BF),
            jax.ShapeDtypeStruct((3, 2, 32, width), BF),
        ],
        compiler_params=params(),
        cost_estimate=cost(4 * tokens * depth * width, 10 * 2**20),
        name="their_grad",
    )(idx, here, plus1, far_a, far_b, minus1, wg, wu)


def my_grad_kernel(acts, wg, wu, mine):
    rows_grad(acts, 0, wg, wu, mine)


def my_grad(acts, wg, wu):
    depth, width = wg.shape
    tokens = acts.shape[1] // 2
    return pl.pallas_call(
        my_grad_kernel,
        in_specs=[VMEM] * 3,
        out_specs=VMEM,
        out_shape=jax.ShapeDtypeStruct((tokens, depth), F32),
        compiler_params=params(),
        cost_estimate=cost(4 * tokens * depth * width, 10 * 2**20),
        name="my_grad",
    )(acts, wg, wu)


def split_kernel(idx, mine, across, *outs):
    for r, out in enumerate(outs):
        at = pl.ds(pl.multiple_of(lax.rem(idx[2] + r, 4) * 64, 64), 64)
        out[...] = (mine[at, :] + across[at, :].astype(F32)).astype(out.dtype)


def split(idx, mine, across):
    shape = (64, mine.shape[1])
    return pl.pallas_call(
        split_kernel,
        in_specs=[SMEM, VMEM, VMEM],
        out_specs=[VMEM] * 4,
        out_shape=[jax.ShapeDtypeStruct(shape, F32)] + [jax.ShapeDtypeStruct(shape, BF)] * 3,
        compiler_params=params(),
        cost_estimate=cost(mine.size, mine.size * 9),
        name="split",
    )(idx, mine, across)


def owned_kernel(own, a, b, c, out):
    total = own[...] + a[...].astype(F32) + b[...].astype(F32) + c[...].astype(F32)
    out[...] = total.astype(out.dtype)


def owned(own, a, b, c, dtype):
    return pl.pallas_call(
        owned_kernel,
        in_specs=[VMEM] * 4,
        out_specs=VMEM,
        out_shape=jax.ShapeDtypeStruct(own.shape, dtype),
        compiler_params=params(),
        cost_estimate=cost(own.size * 4, own.size * 12),
        name="owned",
    )(own, a, b, c)


def part_grads_kernel(m0, m1, acts, gate_out, up_out, xt):
    tokens = m0.shape[1]
    for k, m in enumerate((m0, m1)):
        xt[:, k * tokens : (k + 1) * tokens] = m[0].T
    tile = 256

    @pl.loop(0, acts.shape[2] // tile)
    def _(i):
        at = pl.ds(pl.multiple_of(i * tile, tile), tile)
        gate_out[:, at] = jnp.dot(xt[...], acts[0, :, at], preferred_element_type=F32)
        up_out[:, at] = jnp.dot(xt[...], acts[1, :, at], preferred_element_type=F32)


def part_grads(m0, m1, acts):
    _, tokens, depth = m0.shape
    width = acts.shape[2]
    out = jax.ShapeDtypeStruct((depth, width), F32)
    return pl.pallas_call(
        part_grads_kernel,
        in_specs=[VMEM] * 3,
        out_specs=[VMEM] * 2,
        out_shape=[out, out],
        scratch_shapes=[pltpu.VMEM((depth, 2 * tokens), BF)],
        compiler_params=params(),
        cost_estimate=cost(8 * tokens * depth * width, 8 * 2**20),
        name="part_grads",
    )(m0, m1, acts)


def in_grads_kernel(m0, m1, acts, gate_part, up_part, gate_out, up_out, xt):
    tokens = m0.shape[1]
    tile = gate_out.shape[1]
    i = pl.program_id(0)

    @pl.when(i == 0)
    def _():
        for k, m in enumerate((m0, m1)):
            xt[:, k * tokens : (k + 1) * tokens] = m[0].T

    at = pl.ds(pl.multiple_of(i * tile, tile), tile)
    total = gate_part[:, at] + jnp.dot(xt[...], acts[0, :, at], preferred_element_type=F32)
    gate_out[...] = total.astype(BF)
    total = up_part[:, at] + jnp.dot(xt[...], acts[1, :, at], preferred_element_type=F32)
    up_out[...] = total.astype(BF)


def in_grads(m0, m1, acts, gate_part, up_part):
    _, tokens, depth = m0.shape
    width = acts.shape[2]
    tile = 256
    out = jax.ShapeDtypeStruct((depth, width), BF)
    return pl.pallas_call(
        in_grads_kernel,
        grid=(width // tile,),
        in_specs=[VMEM] * 5,
        out_specs=[pl.BlockSpec((depth, tile), lambda i: (0, i))] * 2,
        out_shape=[out, out],
        scratch_shapes=[pltpu.VMEM((depth, 2 * tokens), BF)],
        compiler_params=params(),
        cost_estimate=cost(8 * tokens * depth * width, 8 * 2**20),
        name="in_grads",
    )(m0, m1, acts, gate_part, up_part)


def gather_hidden(idx, here, other, near, across, out, base):
    for r in range(4):
        for s in range(2):
            start = row_start(idx[0], idx[1], r, s)
            for t in range(2):
                if r:
                    block = (across if s else near)[r - 1, t]
                else:
                    block = other[t] if s else here[4 + t]
                out[pl.ds(base + t * 256 + start, 32), :] = block


def down_grad_kernel(idx, *refs):
    rows, blocks, (out, hidden) = refs[:4], refs[4:12], refs[12:]
    tile = out.shape[0]
    i = pl.program_id(0)

    @pl.when(i == 0)
    def _():
        for k in range(2):
            gather_hidden(idx, *blocks[4 * k : 4 * k + 4], hidden, k * 512)

    at = pl.ds(pl.multiple_of(i * tile, tile), tile)
    g = jnp.concatenate([m[1] for m in rows], axis=0)
    total = jnp.dot(hidden[:, at].T, g, preferred_element_type=F32)
    out[...] = total.astype(BF)


def down_grad(idx, rows, blocks0, blocks1):
    _, tokens, depth = rows[0].shape
    width = blocks0[0].shape[2]
    tile = 256
    return pl.pallas_call(
        down_grad_kernel,
        grid=(width // tile,),
        in_specs=[SMEM] + [VMEM] * 12,
        out_specs=pl.BlockSpec((tile, depth), lambda i: (i, 0)),
        out_shape=jax.ShapeDtypeStruct((width, depth), BF),
        scratch_shapes=[pltpu.VMEM((4 * tokens, width), BF)],
        compiler_params=params(),
        cost_estimate=cost(8 * tokens * depth * width, 4 * 2**20),
        name="down_grad",
    )(idx, *rows, *blocks0, *blocks1)


def body(inputs, upstream, loss_weight, pair_ids, margin, w_gate, w_up, w_down):
    fin = lax.axis_index("fin")
    idx = jnp.stack([fin // 2, fin % 2, lax.axis_index("fout")]).astype(jnp.int32)

    weights = w_gate, w_up, w_down
    m0 = scaled(inputs, upstream, loss_weight, pair_ids, margin)
    m1 = tok_perm(m0, 0, 1)
    m2 = tok_perm(m0, 1, 0)

    def ring(plus, minus):
        return fin_perm(plus, 1, 0), fin_perm(minus, 3, 0)

    def over_y(own, to1, to2, to3):
        return own, y_perm(to2, 2), y_perm(to1, 1), y_perm(to3, 3)

    *out, keep_a, own_a = own_forward(idx, m0, *weights)
    near_a = ring(*out)
    (m1,) = after((m1,), *out)
    *out, keep_b, own_b = forward(idx, m1, *weights)
    near0 = *near_a, *ring(*out)
    owns0 = own_a, own_b
    step0 = pass_on((keep_a, keep_b), near0)
    last0 = ring(*step0)

    (m2,) = after((m2,), *step0)
    m3 = tok_perm(m2, 0, 1)
    *out, keep_a, own_a, cross, stay_a = cross_forward(idx, m2, *weights)
    near_a = ring(*out)
    got_a = fin_perm(cross, 0, 1)
    (m3,) = after((m3,), *out)
    *out, keep_b, own_b, cross, stay_b = cross_forward(idx, m3, *weights)
    near_b = ring(*out)
    got_b = fin_perm(cross, 0, 1)
    last0 = after(last0, *out)
    held0, sent0 = ring_sum(owns0, near0, *last0)
    across0 = fin_perm(sent0, 0, 1)
    got_a, got_b = after((got_a, got_b), sent0)
    *out, keep_c, own_c = cross_sum(stay_a, got_a, stay_b, got_b)
    near1 = *after((*near_a, *near_b), *out), *ring(*out)
    owns1 = own_a, own_b, own_c
    step1 = cross_pass_on((keep_a, keep_b, keep_c), near1)
    last1 = ring(*step1)

    (across0,) = after((across0,), *step1)
    here0, other0 = gate(held0, across0)
    last1 = after(last1, here0)
    held1, held_g, sent1 = cross_ring_sum(owns1, near1, *last1)
    across1 = fin_perm(sent1, 0, 1)

    (ready,) = after((here0,), sent1)
    minus1, plus1 = ring(ready, ready)
    on_plus, on_minus = minus1[:5], plus1[5:]
    far0 = ring(on_plus, on_minus)
    (across1,) = after((across1,), on_plus, on_minus)
    here1, other1 = cross_gate(held1, held_g, across1)
    side1 = ring(here1, here1)

    far0 = after(far0, here1)
    theirs0, act0, near = their_grad(idx, here0, plus1, *far0, minus1, *weights[:2])
    mine0 = my_grad(act0, *weights[:2])
    core0 = tok_perm(theirs0, 0, 1)
    blocks0 = here0, other0, near, fin_perm(near, 0, 1)
    gate_part, up_part = part_grads(m0, m1, act0)
    (core0,) = after((core0,), gate_part)
    parts0 = split(idx, mine0, core0)
    sums0 = over_y(*parts0)
    side1 = after(side1, parts0[0])
    far1 = ring(side1[0][:5], side1[1][5:])

    far1 = after(far1, *sums0[1:], blocks0[3])
    theirs1, act1, near = their_grad(idx, here1, side1[1], *far1, side1[0], *weights[:2])
    mine1 = my_grad(act1, *weights[:2])
    core1 = tok_perm(theirs1, 0, 1)
    blocks1 = here1, other1, near, fin_perm(near, 0, 1)
    total0 = owned(*after(sums0, act1), F32)
    (core1,) = after((core1,), total0)
    parts1 = split(idx, mine1, core1)
    sums1 = over_y(*parts1)
    (act1,) = after((act1,), parts1[0])
    grad_gate, grad_up = in_grads(m2, m3, act1, gate_part, up_part)
    far = owned(*after(sums1, grad_gate), BF)
    blocks1 = after(blocks1, far)
    far = tok_perm(far, 1, 0)
    grad_down = down_grad(idx, (m0, m1, m2, m3), blocks0, blocks1)
    (far,) = after((far,), grad_down)
    total = total0 + far.astype(F32)
    return (total.astype(BF), grad_gate, grad_up, grad_down)


def solution(mesh):
    placed = (
        P("tok", "fin"),
        P("tok", "fin"),
        P("tok"),
        P("tok"),
        P(),
        P("fin", ("tok", "fout")),
        P("fin", ("tok", "fout")),
        P(("tok", "fout"), "fin"),
    )
    return jax.shard_map(
        body,
        mesh=mesh,
        in_specs=placed,
        out_specs=(
            P(("tok", "fout"), "fin"),
            P("fin", ("tok", "fout")),
            P("fin", ("tok", "fout")),
            P(("tok", "fout"), "fin"),
        ),
        check_vma=False,
    )
```

```python
import jax
import jax.numpy as jnp
from jax import lax
from jax.experimental import pallas as pl
from jax.experimental.pallas import tpu as pltpu
from jax.sharding import PartitionSpec as P

BF = jnp.bfloat16
F32 = jnp.float32
NT = (((1,), (1,)), ((), ()))
VMEM_LIMIT = 16 * 1024 * 1024
FIRST_LIMIT = 56 * 1024 * 1024
SMEM = pl.BlockSpec(memory_space=pltpu.SMEM)
VMEM = pl.BlockSpec(memory_space=pltpu.VMEM)


def params(limit=VMEM_LIMIT):
    return pltpu.CompilerParams(vmem_limit_bytes=limit)


def cost(flops, nbytes):
    return pl.CostEstimate(flops=flops, bytes_accessed=nbytes, transcendentals=0)


def fin_perm(x, dz, dx):
    pairs = [(z * 2 + l, ((z + dz) % 4) * 2 + (l ^ dx)) for z in range(4) for l in range(2)]
    return lax.ppermute(x, "fin", pairs)


def tok_perm(x, dh, dc):
    pairs = [(h * 2 + c, (h ^ dh) * 2 + (c ^ dc)) for h in range(2) for c in range(2)]
    return lax.ppermute(x, "tok", pairs)


def y_perm(x, dy):
    return lax.ppermute(x, "fout", [(y, (y + dy) % 4) for y in range(4)])


def after(x, *done):
    n = len(x)
    return lax.optimization_barrier((*x, *done))[:n]


def row_start(z, lo, r, s):
    return pl.multiple_of((lax.rem(z + r, 4) * 2 + lax.bitwise_xor(lo, s)) * 32, 32)


def scale_kernel(margin, x, up, weight, ids, out):
    tokens = x.shape[0]
    out[0] = x[...]
    pair = ids[...] // 2
    picked = jnp.zeros(pair.shape, F32)
    for p in range(margin.shape[0]):
        picked = jnp.where(pair == p, margin[p], picked)
    side = jnp.where(ids[...] % 2 == 0, -1.0, 1.0)
    row = weight[...].astype(F32) * (side * jax.nn.sigmoid(-picked))
    at = lax.broadcasted_iota(jnp.int32, (tokens, tokens), 0)
    to = lax.broadcasted_iota(jnp.int32, (tokens, tokens), 1)
    column = jnp.sum(jnp.where(at == to, row, 0.0), axis=1, keepdims=True)
    out[1] = (column * up[...].astype(F32)).astype(BF)


def scaled(inputs, upstream, loss_weight, pair_ids, margin):
    tokens, depth = inputs.shape
    tile = depth // 2
    wide = pl.BlockSpec((tokens, tile), lambda i: (0, i))
    row = pl.BlockSpec((1, tokens), lambda i: (0, 0))
    return pl.pallas_call(
        scale_kernel,
        grid=(depth // tile,),
        in_specs=[pl.BlockSpec(memory_space=pltpu.SMEM), wide, wide, row, row],
        out_specs=pl.BlockSpec((2, tokens, tile), lambda i: (0, 0, i)),
        out_shape=jax.ShapeDtypeStruct((2, tokens, depth), BF),
        compiler_params=params(FIRST_LIMIT),
        cost_estimate=cost(4 * tokens * depth, 8 * tokens * depth),
        name="scaled",
    )(margin, inputs, upstream, loss_weight.reshape(1, -1), pair_ids.reshape(1, -1))


def forward_kernel(idx, m, wg, wu, wd, plus, minus, keep, own, acc):
    z, lo = idx[0], idx[1]
    tile = acc.shape[2]

    @pl.loop(0, wg.shape[1] // tile)
    def _(i):
        at = pl.ds(pl.multiple_of(i * tile, tile), tile)
        acc[0] = jnp.dot(m[0], wg[:, at], preferred_element_type=F32)
        acc[1] = jnp.dot(m[0], wu[:, at], preferred_element_type=F32)
        acc[2] = lax.dot_general(m[1], wd[at, :], NT, preferred_element_type=F32)

        def block(r, s):
            return acc[:, pl.ds(row_start(z, lo, r, s), 32), :]

        plus[0, :, :, at] = block(2, 0).astype(BF)
        plus[1, :, :, at] = block(1, 1).astype(BF)
        minus[0, :, :, at] = block(2, 1).astype(BF)
        minus[1, :, :, at] = block(3, 0).astype(BF)
        keep[0, :, :, at] = block(1, 0)
        keep[1, :, :, at] = block(3, 1)
        own[0, :, :, at] = block(0, 0)
        own[1, :, :, at] = block(0, 1)


def forward(idx, m, wg, wu, wd):
    _, tokens, depth = m.shape
    width = wg.shape[1]
    tile = 256
    shape = (2, 3, 32, width)
    return pl.pallas_call(
        forward_kernel,
        in_specs=[SMEM] + [VMEM] * 4,
        out_specs=[VMEM] * 4,
        out_shape=[
            jax.ShapeDtypeStruct(shape, BF),
            jax.ShapeDtypeStruct(shape, BF),
            jax.ShapeDtypeStruct(shape, F32),
            jax.ShapeDtypeStruct(shape, F32),
        ],
        scratch_shapes=[pltpu.VMEM((3, tokens, tile), F32)],
        compiler_params=params(),
        cost_estimate=cost(6 * tokens * depth * width, 5 * 2**20),
        name="forward",
    )(idx, m, wg, wu, wd)


def own_forward_kernel(idx, m, wg, wu, wd, plus, minus, keep, own, hg, hu, acc, sems):
    z, lo = idx[0], idx[1]
    piece = 256
    order = [(k, i) for i in range(wg.shape[0] // piece) for k in range(2)]
    places = (wg, hg), (wu, hu)
    copies = []
    for n, (k, i) in enumerate(order):
        src, dst = places[k]
        at = pl.ds(i * piece, piece)
        copies.append(pltpu.make_async_copy(src.at[at], dst.at[at], sems.at[n]))
    ahead = 4
    for copy in copies[:ahead]:
        copy.start()
    acc[2] = lax.dot_general(m[1], wd[...], NT, preferred_element_type=F32)
    for n, (k, i) in enumerate(order):
        copies[n].wait()
        if n + ahead < len(copies):
            copies[n + ahead].start()
        at = slice(i * piece, (i + 1) * piece)
        part = jnp.dot(m[0, :, at], places[k][1][at, :], preferred_element_type=F32)
        acc[k] = acc[k] + part if i else part

    def block(r, s):
        return acc[:, pl.ds(row_start(z, lo, r, s), 32), :]

    plus[0] = block(2, 0).astype(BF)
    plus[1] = block(1, 1).astype(BF)
    minus[0] = block(2, 1).astype(BF)
    minus[1] = block(3, 0).astype(BF)
    keep[0] = block(1, 0)
    keep[1] = block(3, 1)
    own[0] = block(0, 0)
    own[1] = block(0, 1)


def own_forward(idx, m, wg, wu, wd):
    _, tokens, depth = m.shape
    width = wg.shape[1]
    shape = (2, 3, 32, width)
    return pl.pallas_call(
        own_forward_kernel,
        in_specs=[SMEM, VMEM] + [pl.BlockSpec(memory_space=pl.ANY)] * 2 + [VMEM],
        out_specs=[VMEM] * 4,
        out_shape=[
            jax.ShapeDtypeStruct(shape, BF),
            jax.ShapeDtypeStruct(shape, BF),
            jax.ShapeDtypeStruct(shape, F32),
            jax.ShapeDtypeStruct(shape, F32),
        ],
        scratch_shapes=[
            pltpu.VMEM(wg.shape, BF),
            pltpu.VMEM(wu.shape, BF),
            pltpu.VMEM((3, tokens, width), F32),
            pltpu.SemaphoreType.DMA((8,)),
        ],
        compiler_params=params(50 * 2**20),
        cost_estimate=cost(6 * tokens * depth * width, 11 * 2**20),
        name="own_forward",
    )(idx, m, wg, wu, wd)


def pass_on_kernel(*refs):
    plus, minus = refs[6:]
    for t in range(2):
        keep, from_minus, from_plus = refs[3 * t : 3 * t + 3]
        plus[:, t] = (keep[0] + from_minus[0].astype(F32)).astype(BF)
        minus[:, t] = (keep[1] + from_plus[0].astype(F32)).astype(BF)


def pass_on(keeps, nears):
    _, three, rows, width = keeps[0].shape
    shape = jax.ShapeDtypeStruct((three, 2, rows, width), BF)
    size = 2 * keeps[0].size
    return pl.pallas_call(
        pass_on_kernel,
        out_shape=[shape, shape],
        compiler_params=params(),
        cost_estimate=cost(size, size * 8),
        name="pass_on",
    )(keeps[0], *nears[:2], keeps[1], *nears[2:])


def ring_sum_kernel(*refs):
    last_minus, last_plus, held, sent = refs[6:]
    for t in range(2):
        own, from_minus, from_plus = refs[3 * t : 3 * t + 3]
        held[0, :, t] = own[0] + from_plus[1].astype(F32) + last_minus[:, t].astype(F32)
        held[1, :, t] = own[1] + from_minus[1].astype(F32) + last_plus[:, t].astype(F32)
    sent[...] = held[...].astype(BF)


def ring_sum(owns, nears, last_minus, last_plus):
    _, three, rows, width = owns[0].shape
    shape = (2, three, 2, rows, width)
    size = 2 * owns[0].size
    return pl.pallas_call(
        ring_sum_kernel,
        out_shape=[jax.ShapeDtypeStruct(shape, F32), jax.ShapeDtypeStruct(shape, BF)],
        compiler_params=params(),
        cost_estimate=cost(size * 4, size * 14),
        name="ring_sum",
    )(owns[0], *nears[:2], owns[1], *nears[2:], last_minus, last_plus)


def cross_forward_kernel(idx, m, wg, wu, wd, plus, minus, keep, own, cross, stay, acc):
    z, lo = idx[0], idx[1]
    tile = acc.shape[2]

    @pl.loop(0, wg.shape[1] // tile)
    def _(i):
        at = pl.ds(pl.multiple_of(i * tile, tile), tile)
        acc[0] = jnp.dot(m[0], wg[:, at], preferred_element_type=F32)
        acc[1] = jnp.dot(m[0], wu[:, at], preferred_element_type=F32)
        acc[2] = lax.dot_general(m[1], wd[at, :], NT, preferred_element_type=F32)

        def block(r, s):
            return acc[:2, pl.ds(row_start(z, lo, r, s), 32), :]

        plus[0, :, :, at] = block(2, 0).astype(BF)
        plus[1, :, :, at] = block(1, 1).astype(BF)
        minus[0, :, :, at] = block(2, 1).astype(BF)
        minus[1, :, :, at] = block(3, 0).astype(BF)
        keep[0, :, :, at] = block(1, 0)
        keep[1, :, :, at] = block(3, 1)
        own[0, :, :, at] = block(0, 0)
        own[1, :, :, at] = block(0, 1)
        for r in range(4):
            stay[r, :, at] = acc[2, pl.ds(row_start(z, lo, r, 0), 32), :]
            cross[r, :, at] = acc[2, pl.ds(row_start(z, lo, r, 1), 32), :].astype(BF)


def cross_forward(idx, m, wg, wu, wd):
    _, tokens, depth = m.shape
    width = wg.shape[1]
    tile = 256
    shape = (2, 2, 32, width)
    return pl.pallas_call(
        cross_forward_kernel,
        in_specs=[SMEM] + [VMEM] * 4,
        out_specs=[VMEM] * 6,
        out_shape=[
            jax.ShapeDtypeStruct(shape, BF),
            jax.ShapeDtypeStruct(shape, BF),
            jax.ShapeDtypeStruct(shape, F32),
            jax.ShapeDtypeStruct(shape, F32),
            jax.ShapeDtypeStruct((4, 32, width), BF),
            jax.ShapeDtypeStruct((4, 32, width), F32),
        ],
        scratch_shapes=[pltpu.VMEM((3, tokens, tile), F32)],
        compiler_params=params(),
        cost_estimate=cost(6 * tokens * depth * width, 5 * 2**20),
        name="cross_forward",
    )(idx, m, wg, wu, wd)


def cross_sum_kernel(stay0, got0, stay1, got1, plus, minus, keep, own):
    def total(t, r):
        stay, got = (stay0, got0) if t == 0 else (stay1, got1)
        return stay[r] + got[r].astype(F32)

    plus[0] = total(0, 2).astype(BF)
    plus[1] = total(1, 1).astype(BF)
    minus[0] = total(1, 2).astype(BF)
    minus[1] = total(0, 3).astype(BF)
    keep[0] = total(0, 1)
    keep[1] = total(1, 3)
    own[0] = total(0, 0)
    own[1] = total(1, 0)


def cross_sum(stay0, got0, stay1, got1):
    shape = (2, *stay0.shape[1:])
    return pl.pallas_call(
        cross_sum_kernel,
        in_specs=[VMEM] * 4,
        out_specs=[VMEM] * 4,
        out_shape=[
            jax.ShapeDtypeStruct(shape, BF),
            jax.ShapeDtypeStruct(shape, BF),
            jax.ShapeDtypeStruct(shape, F32),
            jax.ShapeDtypeStruct(shape, F32),
        ],
        compiler_params=params(),
        cost_estimate=cost(stay0.size * 2, stay0.size * 18),
        name="cross_sum",
    )(stay0, got0, stay1, got1)


def cross_pass_on_kernel(*refs):
    (keep, from_minus, from_plus), (plus, minus) = refs[6:9], refs[9:]
    plus[4] = (keep[0] + from_minus[0].astype(F32)).astype(BF)
    minus[4] = (keep[1] + from_plus[0].astype(F32)).astype(BF)
    for t in range(2):
        keep, from_minus, from_plus = refs[3 * t : 3 * t + 3]
        for i in range(2):
            plus[2 * i + t] = (keep[0, i] + from_minus[0, i].astype(F32)).astype(BF)
            minus[2 * i + t] = (keep[1, i] + from_plus[0, i].astype(F32)).astype(BF)


def cross_pass_on(keeps, nears):
    _, _, rows, width = keeps[0].shape
    shape = jax.ShapeDtypeStruct((5, rows, width), BF)
    size = 10 * rows * width
    return pl.pallas_call(
        cross_pass_on_kernel,
        in_specs=[VMEM] * 9,
        out_specs=[VMEM] * 2,
        out_shape=[shape, shape],
        compiler_params=params(),
        cost_estimate=cost(size, size * 8),
        name="cross_pass_on",
    )(keeps[0], *nears[:2], keeps[1], *nears[2:4], keeps[2], *nears[4:])


def cross_ring_sum_kernel(*refs):
    (own_g, minus_g, plus_g), (last_minus, last_plus, held, held_g, sent) = refs[6:9], refs[9:]
    for t in range(2):
        own, from_minus, from_plus = refs[3 * t : 3 * t + 3]
        for i in range(2):
            k = 2 * i + t
            held[k] = own[0, i] + from_plus[1, i].astype(F32) + last_minus[k].astype(F32)
            held[4 + k] = own[1, i] + from_minus[1, i].astype(F32) + last_plus[k].astype(F32)
    held_g[0] = own_g[0] + plus_g[1].astype(F32) + last_minus[4].astype(F32)
    held_g[1] = own_g[1] + minus_g[1].astype(F32) + last_plus[4].astype(F32)
    sent[:8] = held[...].astype(BF)
    sent[8:] = held_g[...].astype(BF)


def cross_ring_sum(owns, nears, last_minus, last_plus):
    _, _, rows, width = owns[0].shape
    size = 10 * rows * width
    return pl.pallas_call(
        cross_ring_sum_kernel,
        in_specs=[VMEM] * 11,
        out_specs=[VMEM] * 3,
        out_shape=[
            jax.ShapeDtypeStruct((8, rows, width), F32),
            jax.ShapeDtypeStruct((2, rows, width), F32),
            jax.ShapeDtypeStruct((10, rows, width), BF),
        ],
        compiler_params=params(),
        cost_estimate=cost(size * 4, size * 14),
        name="cross_ring_sum",
    )(owns[0], *nears[:2], owns[1], *nears[2:4], owns[2], *nears[4:], last_minus, last_plus)


def cross_gate_kernel(held, held_g, across, out, other):
    for half in range(2):
        mine, theirs = 4 * half, 4 * (1 - half)
        pre_gate = held[mine : mine + 2] + across[theirs : theirs + 2].astype(F32)
        pre_up = held[mine + 2 : mine + 4] + across[theirs + 2 : theirs + 4].astype(F32)
        grad_hidden = across[8:].astype(F32) if half else held_g[...]
        put_gate(half, pre_gate, pre_up, grad_hidden, out, other)


def cross_gate(held, held_g, across):
    _, rows, width = held.shape
    return pl.pallas_call(
        cross_gate_kernel,
        in_specs=[VMEM] * 3,
        out_specs=[VMEM] * 2,
        out_shape=[
            jax.ShapeDtypeStruct((10, rows, width), BF),
            jax.ShapeDtypeStruct((2, rows, width), BF),
        ],
        compiler_params=params(),
        cost_estimate=cost(held.size * 8, held.size * 8),
        name="cross_gate",
    )(held, held_g, across)


def put_gate(half, pre_gate, pre_up, grad_hidden, out, other):
    s = jax.nn.sigmoid(pre_gate)
    activated = pre_gate * s
    first = 6 * half
    out[first : first + 2] = (
        grad_hidden * pre_up * s * (1.0 + pre_gate * (1.0 - s))
    ).astype(BF)
    out[first + 2 : first + 4] = (grad_hidden * activated).astype(BF)
    hidden = (activated * pre_up).astype(BF)
    if half:
        other[...] = hidden
    else:
        out[4:6] = hidden


def gate_kernel(held, across, out, other):
    for half in range(2):
        pre_gate, pre_up, grad_hidden = (
            held[half, i] + across[1 - half, i].astype(F32) for i in range(3)
        )
        put_gate(half, pre_gate, pre_up, grad_hidden, out, other)


def gate(held, across):
    _, _, two, rows, width = held.shape
    return pl.pallas_call(
        gate_kernel,
        in_specs=[VMEM] * 2,
        out_specs=[VMEM] * 2,
        out_shape=[
            jax.ShapeDtypeStruct((10, rows, width), BF),
            jax.ShapeDtypeStruct((two, rows, width), BF),
        ],
        compiler_params=params(),
        cost_estimate=cost(held.size * 8, held.size * 8),
        name="gate",
    )(held, across)


def their_grad_kernel(idx, here, plus1, far_a, far_b, minus1, wg, wu, theirs, acts, hidden):
    z, lo = idx[0], idx[1]
    tokens = acts.shape[1] // 2
    for r, s, block in (
        (0, 0, here.at[:4]),
        (0, 1, here.at[6:]),
        (1, 0, plus1.at[:4]),
        (1, 1, plus1.at[6:]),
        (2, 0, far_a.at[:4]),
        (2, 1, far_b.at[1:]),
        (3, 0, minus1.at[:4]),
        (3, 1, minus1.at[6:]),
    ):
        start = row_start(z, lo, r, s)
        for i in range(2):
            for t in range(2):
                acts[i, pl.ds(t * tokens + start, 32), :] = block[2 * i + t]
    hidden[0] = plus1[4:6]
    hidden[1, 0] = far_a[4]
    hidden[1, 1] = far_b[0]
    hidden[2] = minus1[4:6]

    rows_grad(acts, tokens, wg, wu, theirs)


def rows_grad(acts, first, wg, wu, out):
    rows, tile = out.shape[0], 256

    @pl.loop(0, wg.shape[0] // tile)
    def _(i):
        at = pl.ds(pl.multiple_of(i * tile, tile), tile)
        total = lax.dot_general(
            acts[0, first : first + rows], wg[at, :], NT, preferred_element_type=F32
        )
        total += lax.dot_general(
            acts[1, first : first + rows], wu[at, :], NT, preferred_element_type=F32
        )
        out[:, at] = total.astype(out.dtype)


def their_grad(idx, here, plus1, far_a, far_b, minus1, wg, wu):
    depth, width = wg.shape
    tokens = 256
    return pl.pallas_call(
        their_grad_kernel,
        in_specs=[SMEM] + [VMEM] * 7,
        out_specs=[VMEM] * 3,
        out_shape=[
            jax.ShapeDtypeStruct((tokens, depth), BF),
            jax.ShapeDtypeStruct((2, 2 * tokens, width), BF),
            jax.ShapeDtypeStruct((3, 2, 32, width), BF),
        ],
        compiler_params=params(),
        cost_estimate=cost(4 * tokens * depth * width, 10 * 2**20),
        name="their_grad",
    )(idx, here, plus1, far_a, far_b, minus1, wg, wu)


def my_grad_kernel(acts, wg, wu, mine):
    rows_grad(acts, 0, wg, wu, mine)


def my_grad(acts, wg, wu):
    depth, width = wg.shape
    tokens = acts.shape[1] // 2
    return pl.pallas_call(
        my_grad_kernel,
        in_specs=[VMEM] * 3,
        out_specs=VMEM,
        out_shape=jax.ShapeDtypeStruct((tokens, depth), F32),
        compiler_params=params(),
        cost_estimate=cost(4 * tokens * depth * width, 10 * 2**20),
        name="my_grad",
    )(acts, wg, wu)


def split_kernel(idx, mine, across, *outs):
    for r, out in enumerate(outs):
        at = pl.ds(pl.multiple_of(lax.rem(idx[2] + r, 4) * 64, 64), 64)
        out[...] = (mine[at, :] + across[at, :].astype(F32)).astype(out.dtype)


def split(idx, mine, across):
    shape = (64, mine.shape[1])
    return pl.pallas_call(
        split_kernel,
        in_specs=[SMEM, VMEM, VMEM],
        out_specs=[VMEM] * 4,
        out_shape=[jax.ShapeDtypeStruct(shape, F32)] + [jax.ShapeDtypeStruct(shape, BF)] * 3,
        compiler_params=params(),
        cost_estimate=cost(mine.size, mine.size * 9),
        name="split",
    )(idx, mine, across)


def owned_kernel(own, a, b, c, out):
    total = own[...] + a[...].astype(F32) + b[...].astype(F32) + c[...].astype(F32)
    out[...] = total.astype(out.dtype)


def owned(own, a, b, c, dtype):
    return pl.pallas_call(
        owned_kernel,
        in_specs=[VMEM] * 4,
        out_specs=VMEM,
        out_shape=jax.ShapeDtypeStruct(own.shape, dtype),
        compiler_params=params(),
        cost_estimate=cost(own.size * 4, own.size * 12),
        name="owned",
    )(own, a, b, c)


def part_grads_kernel(m0, m1, acts, gate_out, up_out, xt):
    tokens = m0.shape[1]
    for k, m in enumerate((m0, m1)):
        xt[:, k * tokens : (k + 1) * tokens] = m[0].T
    tile = 256

    @pl.loop(0, acts.shape[2] // tile)
    def _(i):
        at = pl.ds(pl.multiple_of(i * tile, tile), tile)
        gate_out[:, at] = jnp.dot(xt[...], acts[0, :, at], preferred_element_type=F32)
        up_out[:, at] = jnp.dot(xt[...], acts[1, :, at], preferred_element_type=F32)


def part_grads(m0, m1, acts):
    _, tokens, depth = m0.shape
    width = acts.shape[2]
    out = jax.ShapeDtypeStruct((depth, width), F32)
    return pl.pallas_call(
        part_grads_kernel,
        in_specs=[VMEM] * 3,
        out_specs=[VMEM] * 2,
        out_shape=[out, out],
        scratch_shapes=[pltpu.VMEM((depth, 2 * tokens), BF)],
        compiler_params=params(),
        cost_estimate=cost(8 * tokens * depth * width, 8 * 2**20),
        name="part_grads",
    )(m0, m1, acts)


def in_grads_kernel(m0, m1, acts, gate_part, up_part, gate_out, up_out, xt):
    tokens = m0.shape[1]
    tile = gate_out.shape[1]
    i = pl.program_id(0)

    @pl.when(i == 0)
    def _():
        for k, m in enumerate((m0, m1)):
            xt[:, k * tokens : (k + 1) * tokens] = m[0].T

    at = pl.ds(pl.multiple_of(i * tile, tile), tile)
    total = gate_part[:, at] + jnp.dot(xt[...], acts[0, :, at], preferred_element_type=F32)
    gate_out[...] = total.astype(BF)
    total = up_part[:, at] + jnp.dot(xt[...], acts[1, :, at], preferred_element_type=F32)
    up_out[...] = total.astype(BF)


def in_grads(m0, m1, acts, gate_part, up_part):
    _, tokens, depth = m0.shape
    width = acts.shape[2]
    tile = 256
    out = jax.ShapeDtypeStruct((depth, width), BF)
    return pl.pallas_call(
        in_grads_kernel,
        grid=(width // tile,),
        in_specs=[VMEM] * 5,
        out_specs=[pl.BlockSpec((depth, tile), lambda i: (0, i))] * 2,
        out_shape=[out, out],
        scratch_shapes=[pltpu.VMEM((depth, 2 * tokens), BF)],
        compiler_params=params(),
        cost_estimate=cost(8 * tokens * depth * width, 8 * 2**20),
        name="in_grads",
    )(m0, m1, acts, gate_part, up_part)


def gather_hidden(idx, here, other, near, across, out, base):
    for r in range(4):
        for s in range(2):
            start = row_start(idx[0], idx[1], r, s)
            for t in range(2):
                if r:
                    block = (across if s else near)[r - 1, t]
                else:
                    block = other[t] if s else here[4 + t]
                out[pl.ds(base + t * 256 + start, 32), :] = block


def down_grad_kernel(idx, *refs):
    rows, blocks, (out, hidden) = refs[:4], refs[4:12], refs[12:]
    tile = out.shape[0]
    i = pl.program_id(0)

    @pl.when(i == 0)
    def _():
        for k in range(2):
            gather_hidden(idx, *blocks[4 * k : 4 * k + 4], hidden, k * 512)

    at = pl.ds(pl.multiple_of(i * tile, tile), tile)
    g = jnp.concatenate([m[1] for m in rows], axis=0)
    total = jnp.dot(hidden[:, at].T, g, preferred_element_type=F32)
    out[...] = total.astype(BF)


def down_grad(idx, rows, blocks0, blocks1):
    _, tokens, depth = rows[0].shape
    width = blocks0[0].shape[2]
    tile = 256
    return pl.pallas_call(
        down_grad_kernel,
        grid=(width // tile,),
        in_specs=[SMEM] + [VMEM] * 12,
        out_specs=pl.BlockSpec((tile, depth), lambda i: (i, 0)),
        out_shape=jax.ShapeDtypeStruct((width, depth), BF),
        scratch_shapes=[pltpu.VMEM((4 * tokens, width), BF)],
        compiler_params=params(),
        cost_estimate=cost(8 * tokens * depth * width, 4 * 2**20),
        name="down_grad",
    )(idx, *rows, *blocks0, *blocks1)


def body(inputs, upstream, loss_weight, pair_ids, margin, w_gate, w_up, w_down):
    fin = lax.axis_index("fin")
    idx = jnp.stack([fin // 2, fin % 2, lax.axis_index("fout")]).astype(jnp.int32)

    weights = w_gate, w_up, w_down
    m0 = scaled(inputs, upstream, loss_weight, pair_ids, margin)
    m1 = tok_perm(m0, 0, 1)
    m2 = tok_perm(m0, 1, 0)

    def ring(plus, minus):
        return fin_perm(plus, 1, 0), fin_perm(minus, 3, 0)

    def over_y(own, to1, to2, to3):
        return own, y_perm(to2, 2), y_perm(to1, 1), y_perm(to3, 3)

    *out, keep_a, own_a = own_forward(idx, m0, *weights)
    near_a = ring(*out)
    (m1,) = after((m1,), *out)
    *out, keep_b, own_b = forward(idx, m1, *weights)
    near0 = *near_a, *ring(*out)
    owns0 = own_a, own_b
    step0 = pass_on((keep_a, keep_b), near0)
    last0 = ring(*step0)

    (m2,) = after((m2,), *step0)
    m3 = tok_perm(m2, 0, 1)
    *out, keep_a, own_a, cross, stay_a = cross_forward(idx, m2, *weights)
    near_a = ring(*out)
    got_a = fin_perm(cross, 0, 1)
    (m3,) = after((m3,), *out)
    *out, keep_b, own_b, cross, stay_b = cross_forward(idx, m3, *weights)
    near_b = ring(*out)
    got_b = fin_perm(cross, 0, 1)
    last0 = after(last0, *out)
    held0, sent0 = ring_sum(owns0, near0, *last0)
    across0 = fin_perm(sent0, 0, 1)
    got_a, got_b = after((got_a, got_b), sent0)
    *out, keep_c, own_c = cross_sum(stay_a, got_a, stay_b, got_b)
    near1 = *after((*near_a, *near_b), *out), *ring(*out)
    owns1 = own_a, own_b, own_c
    step1 = cross_pass_on((keep_a, keep_b, keep_c), near1)
    last1 = ring(*step1)

    (across0,) = after((across0,), *step1)
    here0, other0 = gate(held0, across0)
    last1 = after(last1, here0)
    held1, held_g, sent1 = cross_ring_sum(owns1, near1, *last1)
    across1 = fin_perm(sent1, 0, 1)

    (ready,) = after((here0,), *last1)
    minus1, plus1 = ring(ready, ready)
    on_plus, on_minus = minus1[:5], plus1[5:]
    far0 = ring(on_plus, on_minus)
    (across1,) = after((across1,), on_plus, on_minus)
    here1, other1 = cross_gate(held1, held_g, across1)
    side1 = ring(here1, here1)

    far0 = after(far0, here1)
    theirs0, act0, near = their_grad(idx, here0, plus1, *far0, minus1, *weights[:2])
    mine0 = my_grad(act0, *weights[:2])
    core0 = tok_perm(theirs0, 0, 1)
    blocks0 = here0, other0, near, fin_perm(near, 0, 1)
    gate_part, up_part = part_grads(m0, m1, act0)
    (core0,) = after((core0,), gate_part)
    parts0 = split(idx, mine0, core0)
    sums0 = over_y(*parts0)
    side1 = after(side1, parts0[0])
    far1 = ring(side1[0][:5], side1[1][5:])

    far1 = after(far1, *sums0[1:], blocks0[3])
    theirs1, act1, near = their_grad(idx, here1, side1[1], *far1, side1[0], *weights[:2])
    mine1 = my_grad(act1, *weights[:2])
    core1 = tok_perm(theirs1, 0, 1)
    blocks1 = here1, other1, near, fin_perm(near, 0, 1)
    total0 = owned(*after(sums0, act1), F32)
    (core1,) = after((core1,), total0)
    parts1 = split(idx, mine1, core1)
    sums1 = over_y(*parts1)
    (act1,) = after((act1,), parts1[0])
    grad_gate, grad_up = in_grads(m2, m3, act1, gate_part, up_part)
    far = owned(*after(sums1, grad_gate), BF)
    blocks1 = after(blocks1, far)
    far = tok_perm(far, 1, 0)
    grad_down = down_grad(idx, (m0, m1, m2, m3), blocks0, blocks1)
    (far,) = after((far,), grad_down)
    total = total0 + far.astype(F32)
    return (total.astype(BF), grad_gate, grad_up, grad_down)


def solution(mesh):
    placed = (
        P("tok", "fin"),
        P("tok", "fin"),
        P("tok"),
        P("tok"),
        P(),
        P("fin", ("tok", "fout")),
        P("fin", ("tok", "fout")),
        P(("tok", "fout"), "fin"),
    )
    return jax.shard_map(
        body,
        mesh=mesh,
        in_specs=placed,
        out_specs=(
            P(("tok", "fout"), "fin"),
            P("fin", ("tok", "fout")),
            P("fin", ("tok", "fout")),
            P(("tok", "fout"), "fin"),
        ),
        check_vma=False,
    )
```
